512 devices in a mesh: gx: 4 (over y), gy: 4 (over x), gz: 32 (over z, core).
Axes of the slice: x: 4, y: 4, z: 16, core: 2. Of those that a mesh axis runs over, the one named last changes fastest.
Arguments:
- multipoles: float32 [121, 524288], P(None, ('gx', 'gy', 'gz')), may hold values from -6 to 6
- sources: int32 [16384, 1024], P(('gx', 'gy', 'gz')), may hold values from 0 to 2559
- halo_cells: int32 [3072, 256], P(('gx', 'gy', 'gz')), may hold values from 0 to 1023
- m2l_ops: float32 [32, 121, 121], replicated, may hold values from -0.09375 to 0.09375
- cell_up: float32 [8, 121, 121], replicated, may hold values from -0.015625 to 0.015625
- cell_down: float32 [8, 121, 121], replicated, may hold values from -0.5 to 0.5
- side_ops: float32 [3, 2, 121, 121], replicated, may hold values from -0.375 to 0.375
Outputs:
- local_fields: float32 [121, 524288], P(None, ('gx', 'gy', 'gz'))
The draws below stay inside these ranges and needn't reach their ends.
Inputs may be any that keep to these rules, and one draw needn't show every extreme that they name: `sources`: slot of a device's own cells or its received face cells.
All inputs are finite; a program needn't handle non-finite values.
Results may differ from the reference program's by a relative error of at most 0.0003.
Values sent between devices are 32-bit elements; how exact they have to be, the bound alone decides.
A program may use at most 64 MiB of HBM per device.

```python
import jax
import jax.numpy as jnp
from jax import lax

COEF = 121
OPS = 32
CELLS = 1024
HALO = 256
PER_OP = 1024
SECTIONS = 9
ALL_CELLS = 524288
LIST_ROWS = 16384
FACE_ROWS = 3072
N_GX = 4
N_GY = 4
N_GZ = 32


def with_ends(drawn, key, least, largest):
    shape = drawn.shape
    index_at = [jax.random.randint(jax.random.fold_in(key, axis), (), 0, shape[axis]) for axis in range(len(shape))]
    drawn = drawn.at[tuple(index_at)].set(least)
    longest = shape.index(max(shape))
    index_at[longest] = (index_at[longest] + 1) % shape[longest]
    return drawn.at[tuple(index_at)].set(largest)


def steps_of(key, extent, split, smallest, high):
    gain = 1.0
    for dim, parts in split:
        steps = jax.random.uniform(jax.random.fold_in(jax.random.fold_in(key, 6), dim), (parts,), jnp.float32, smallest / len(split), high / len(split))
        gain = gain * jnp.repeat(jnp.exp(steps), extent[dim] // parts).reshape((-1,) + (1,) * (len(extent) - 1 - dim))
    return gain


def bell_draw(rng, shape, scale, most, shards=(), kind=jnp.bfloat16):
    gain = steps_of(rng, shape, shards, -0.22, 0.18) if shards else 1.0
    array = jax.random.normal(rng, shape, jnp.float32) * scale * gain
    return jnp.minimum(jnp.maximum(array, -most), most).astype(kind)


def setup_inputs(seed: int = 0) -> dict:
    key_of = jax.random.split(jax.random.key(seed), 8)
    multipoles = bell_draw(key_of[0], (COEF, ALL_CELLS), 1.0, 6.0, ((1, 512),), jnp.float32)
    sources = with_ends(jax.random.randint(key_of[1], (LIST_ROWS, PER_OP), 0, CELLS + 6 * HALO), jax.random.fold_in(key_of[1], 1), 0, (CELLS + 6 * HALO) - 1).astype(jnp.int32)
    halo_cells = with_ends(jax.random.randint(key_of[2], (FACE_ROWS, HALO), 0, CELLS), jax.random.fold_in(key_of[2], 1), 0, CELLS - 1).astype(jnp.int32)
    m2l_ops = bell_draw(key_of[3], (OPS, COEF, COEF), (COEF * OPS) ** -0.5, 0.09375, (), jnp.float32)
    cell_up = bell_draw(key_of[4], (8, COEF, COEF), (COEF * CELLS) ** -0.5, 0.015625, (), jnp.float32)
    cell_down = bell_draw(key_of[5], (8, COEF, COEF), COEF ** -0.5, 0.5, (), jnp.float32)
    side_ops = bell_draw(key_of[6], (3, 2, COEF, COEF), (2 * COEF) ** -0.5, 0.375, (), jnp.float32)
    return dict(multipoles=multipoles, sources=sources, halo_cells=halo_cells, m2l_ops=m2l_ops, cell_up=cell_up, cell_down=cell_down, side_ops=side_ops)


HIGHEST = lax.Precision.HIGHEST


def reference(multipoles, sources, halo_cells, m2l_ops, cell_up, cell_down, side_ops):
    device_count = N_GX * N_GY * N_GZ
    num_coef = multipoles.shape[0]
    cell_grid = multipoles.reshape(num_coef, device_count, CELLS)
    class_sums = cell_grid.reshape(num_coef, device_count, CELLS // 8, 8).sum(axis=2)
    box_values = jnp.einsum('ocd,dno->cn', cell_up, class_sums, precision=HIGHEST)
    device_ids = jnp.arange(device_count, dtype=jnp.int32)
    far_list = []
    for level_bit in range(SECTIONS):
        box_count = box_values.shape[1]
        paired = box_values.reshape(num_coef, box_count // 2, 2)
        partner = paired[:, :, ::-1].reshape(num_coef, box_count)
        side_bit = jnp.arange(box_count, dtype=jnp.int32) % 2
        lower_far = jnp.dot(side_ops[1, 0], partner, precision=HIGHEST)
        upper_far = jnp.dot(side_ops[1, 1], partner, precision=HIGHEST)
        far_field = jnp.where(side_bit[None, :] == 0, lower_far, upper_far)
        far_list.append(far_field[:, device_ids // (2 ** level_bit)])
        box_values = jnp.dot(side_ops[0, 0], paired[:, :, 0], precision=HIGHEST) + jnp.dot(side_ops[0, 1], paired[:, :, 1], precision=HIGHEST)
    local_field = jnp.zeros((num_coef, device_count), jnp.float32)
    for level_bit in reversed(range(SECTIONS)):
        side_bit = (device_ids // (2 ** level_bit)) % 2
        lower_shift = jnp.dot(side_ops[2, 0], local_field, precision=HIGHEST)
        upper_shift = jnp.dot(side_ops[2, 1], local_field, precision=HIGHEST)
        local_field = jnp.where(side_bit[None, :] == 0, lower_shift, upper_shift) + far_list[level_bit]
    shifted = jnp.einsum('ocd,dn->cno', cell_down, local_field, precision=HIGHEST)
    halo_table = halo_cells.reshape(device_count, 6, HALO)
    source_table = sources.reshape(device_count, OPS, PER_OP)
    strides = (N_GY * N_GZ, N_GZ, 1)
    extents = (N_GX, N_GY, N_GZ)

    def device_terms(device):
        blocks = [lax.dynamic_index_in_dim(cell_grid, device, 1, keepdims=False)]
        for axis_number in range(3):
            position = (device // strides[axis_number]) % extents[axis_number]
            for offset, face_slot in ((-1, 1), (1, 0)):
                present = (position + offset >= 0) & (position + offset < extents[axis_number])
                neighbour = jnp.clip(device + offset * strides[axis_number], 0, device_count - 1).astype(jnp.int32)
                columns = lax.dynamic_index_in_dim(cell_grid, neighbour, 1, keepdims=False)
                face_ids = halo_table[neighbour, 2 * axis_number + face_slot]
                blocks.append(jnp.take(columns, face_ids, axis=1) * present.astype(jnp.float32))
        source_pool = jnp.concatenate(blocks, axis=1)
        picked = jnp.take(source_pool, source_table[device].reshape(-1), axis=1).reshape(num_coef, OPS, PER_OP)
        return jnp.einsum('kcd,dkn->cn', m2l_ops, picked, precision=HIGHEST)

    near_field = lax.map(device_terms, device_ids)
    near_field = jnp.transpose(near_field, (1, 0, 2))
    spread = jnp.broadcast_to(shifted[:, :, None, :], (num_coef, device_count, CELLS // 8, 8)).reshape(num_coef, device_count, CELLS)
    result_field = near_field + spread
    return result_field.reshape(num_coef, device_count * CELLS)
```

```python
import functools

import jax
import jax.numpy as jnp
from jax import lax
from jax.experimental import pallas as pl
from jax.experimental.pallas import tpu as pltpu
from jax.sharding import PartitionSpec as P

F32, BF16 = jnp.float32, jnp.bfloat16
MESH = pl.DeviceIdType.MESH
NT = (((1,), (1,)), ((), ()))
AXES = ("gx", "gy", "gz")


def split(x):
    hi = x.astype(BF16)
    return hi, (x - hi.astype(F32)).astype(BF16)


def nt(a, b):
    return lax.dot_general(a, b, NT, preferred_element_type=F32)


def dot3(x, wide, narrow):
    hi, lo = split(x)
    return nt(hi, wide) + (nt(lo, wide) + nt(hi, narrow))


def pick8(table, index_of, sub):
    block = None
    for s in range(8):
        row = jnp.broadcast_to(table[pl.ds(index_of(s), 1), :], (8, 128))
        block = row if block is None else jnp.where(sub == s, row, block)
    return block


def kernel(
    sizes, mult, sources, halo, m2l, up, down, side, out,
    cells, own, pool, faces, src_s, halo_s, m2l_v, up_v, down_v, side_v,
    near_w, up_w, down_w, merge_w, cross_w, shift_w, acc,
    mine, line, plane, boxes, sibs, far,
    in_sem, src_sem, face_send, face_recv, line_send, line_recv, plane_send, plane_recv,
):
    coef, ncell, ops, nhalo, ngx, ngy, ngz = sizes
    nplane = ngx * ngy
    gx, gy, gz = (lax.axis_index(a) for a in AXES)
    place = gx * ngy + gy
    me = place * ngz + gz
    zero = lax.shift_right_logical(me, 24)
    offs = tuple(zero + j for j in range(8))
    sub = lax.broadcasted_iota(jnp.int32, (8, 128), 0)

    loads = [
        pltpu.make_async_copy(mult, cells, in_sem.at[0]),
        pltpu.make_async_copy(halo, halo_s, in_sem.at[1]),
        pltpu.make_async_copy(up, up_v, in_sem.at[2]),
        pltpu.make_async_copy(side, side_v, in_sem.at[3]),
        pltpu.make_async_copy(m2l, m2l_v, in_sem.at[4]),
        pltpu.make_async_copy(down, down_v, in_sem.at[5]),
    ]
    for load in loads:
        load.start()

    def source_tile(t):
        g, q = lax.div(t, ncell // 128), lax.rem(t, ncell // 128)
        return pltpu.make_async_copy(
            sources.at[pl.ds(pl.multiple_of(g * 8, 8), 8), pl.ds(pl.multiple_of(q * 128, 128), 128)],
            src_s.at[t],
            src_sem.at[t],
        )

    tiles = ops // 8 * (ncell // 128)

    barrier = pltpu.get_barrier_semaphore()

    def in_line(j):
        return {"gz": lax.rem(gz + j, ngz)}

    def in_plane(j):
        other = lax.rem(place + j, nplane)
        return {"gx": lax.div(other, ngy), "gy": lax.rem(other, ngy)}

    def greet(device_of):
        def one(j, c):
            pl.semaphore_signal(barrier, inc=1, device_id=device_of(j), device_id_type=MESH)
            return c

        return one

    lax.fori_loop(1, ngz, greet(in_line), 0)
    lax.fori_loop(1, nplane, greet(in_plane), 0)

    loads[0].wait()
    for b in range(ncell // 128):
        block = jnp.concatenate(
            [cells[:, b * 128 : (b + 1) * 128], jnp.zeros((128 - coef, 128), F32)], axis=0
        ).T
        own[b * 128 : (b + 1) * 128, :] = block
        pool[b * 128 : (b + 1) * 128, :] = block

    loads[1].wait()
    neighbours = (
        (gx, ngx, lambda i: {"gx": i}),
        (gy, ngy, lambda i: {"gy": i}),
        (gz, ngz, lambda i: {"gz": i}),
    )

    def slot(i):
        return pool.at[pl.ds(ncell + i * nhalo, nhalo)]

    def face_copy(face, land, device):
        return pltpu.make_async_remote_copy(
            src_ref=faces.at[face],
            dst_ref=slot(land),
            send_sem=face_send.at[face],
            recv_sem=face_recv.at[land],
            device_id=device,
            device_id_type=MESH,
        )

    def gather_face(face):
        def part(i, c):
            for r in range(16):
                v = halo_s.at[face, pl.ds(i * 128 + r * 8, 8)]
                faces[face, pl.ds(pl.multiple_of(i * 128 + r * 8, 8), 8), :] = pick8(
                    own, lambda s: v[offs[s]], sub
                )
            return c

        lax.fori_loop(0, nhalo // 128, part, 0)

    gather_face(0)
    gather_face(1)
    pl.semaphore_wait(barrier, ngz - 1 + nplane - 1)
    for a, (at, count, device) in enumerate(neighbours):
        if a:
            gather_face(2 * a)
            gather_face(2 * a + 1)

        @pl.when(at < count - 1)
        def _():
            face_copy(2 * a + 1, 2 * a, device(at + 1)).start()

        @pl.when(at > 0)
        def _():
            face_copy(2 * a, 2 * a + 1, device(at - 1)).start()

        @pl.when(at == 0)
        def _():
            slot(2 * a)[...] = jnp.zeros((nhalo, 128), F32)

        @pl.when(at == count - 1)
        def _():
            slot(2 * a + 1)[...] = jnp.zeros((nhalo, 128), F32)

    def fetch(t, c):
        source_tile(t).start()
        return c

    lax.fori_loop(0, tiles, fetch, 0)

    for w in (up_w, down_w, merge_w, cross_w, shift_w, near_w):
        w[...] = jnp.zeros_like(w)
    loads[2].wait()
    for o in range(8):
        hi, lo = split(up_v[pl.ds(o, coef, 8), :])
        up_w[0, 0:coef, o * 128 : o * 128 + coef] = hi
        up_w[1, 0:coef, o * 128 : o * 128 + coef] = lo

    def add_class(i, total):
        for r in range(16):
            total = total + own[pl.ds(pl.multiple_of(i * 128 + r * 8, 8), 8), :]
        return total

    classes = lax.fori_loop(0, ncell // 128, add_class, jnp.zeros((8, 128), F32))
    flat = jnp.concatenate([classes[o : o + 1, :] for o in range(8)], axis=1)
    box = dot3(jnp.broadcast_to(flat, (8, 1024)), up_w[0], up_w[1])
    mine[0] = box[0:1, :]

    def line_copy(j):
        return pltpu.make_async_remote_copy(
            src_ref=mine.at[0],
            dst_ref=line.at[gz],
            send_sem=line_send.at[j],
            recv_sem=line_recv.at[j],
            device_id=in_line(j),
            device_id_type=MESH,
        )

    def plane_copy(j):
        return pltpu.make_async_remote_copy(
            src_ref=mine.at[1],
            dst_ref=plane.at[place],
            send_sem=plane_send.at[j],
            recv_sem=plane_recv.at[j],
            device_id=in_plane(j),
            device_id_type=MESH,
        )

    def start_all(copy_of):
        def one(j, c):
            copy_of(j).start()
            return c

        return one

    def wait_all(copy_of):
        def one(j, c):
            copy_of(j).wait()
            return c

        return one

    lax.fori_loop(1, ngz, start_all(line_copy), 0)
    line[gz] = box[0:1, :]

    loads[3].wait()
    for b in range(2):
        for a, w in enumerate((merge_w, cross_w, shift_w)):
            hi, lo = split(side_v[a, :, b, :])
            if a == 0:
                w[0, 0:coef, b * 128 : b * 128 + coef] = hi
                w[1, 0:coef, b * 128 : b * 128 + coef] = lo
            else:
                w[b, 0, 0:coef, 0:coef] = hi
                w[b, 1, 0:coef, 0:coef] = lo
    loads[4].wait()

    def split_near(p, c):
        for h in range(2):
            hi, lo = split(m2l_v[pl.ds(p * 2 + h, coef, ops), :])
            near_w[p, 0:coef, h * 128 : h * 128 + coef] = hi
            near_w[p, 128 : 128 + coef, h * 128 : h * 128 + coef] = lo
        return c

    lax.fori_loop(0, ops // 2, split_near, 0)
    loads[5].wait()
    for o in range(8):
        hi, lo = split(down_v[pl.ds(o, coef, 8), :])
        down_w[0, o * 128 : o * 128 + coef, 0:coef] = hi
        down_w[1, o * 128 : o * 128 + coef, 0:coef] = lo
    acc[...] = jnp.zeros_like(acc)
    sibs[...] = jnp.zeros_like(sibs)

    def climb(first, sections, count, index):
        for s in range(sections):
            mask = lax.shift_right_logical(index, s)
            sib = mask + 1 - 2 * lax.rem(mask, 2)
            sibs[first + s : first + s + 1, :] = boxes[pl.ds(sib, 1), :]
            half = count >> (s + 1)
            if half:
                pairs = jnp.concatenate(
                    [boxes[pl.ds(0, half, 2), :], boxes[pl.ds(1, half, 2), :]], axis=1
                )
                boxes[0:half, :] = dot3(pairs, merge_w[0], merge_w[1])

    lax.fori_loop(1, ngz, wait_all(line_copy), 0)
    for i in range(ngz):
        boxes[i : i + 1, :] = line[i]
    line_levels = ngz.bit_length() - 1
    plane_levels = nplane.bit_length() - 1
    climb(0, line_levels, ngz, gz)
    mine[1] = boxes[0:1, :]
    plane[place] = boxes[0:1, :]
    lax.fori_loop(1, nplane, start_all(plane_copy), 0)

    for a, (at, count, device) in enumerate(neighbours):
        @pl.when(at < count - 1)
        def _():
            face_copy(2 * a + 1, 2 * a, device(at + 1)).wait_send()
            face_copy(2 * a, 2 * a + 1, device(at + 1)).wait_recv()

        @pl.when(at > 0)
        def _():
            face_copy(2 * a, 2 * a + 1, device(at - 1)).wait_send()
            face_copy(2 * a + 1, 2 * a, device(at - 1)).wait_recv()

    def arrived(t, c):
        source_tile(t).wait()
        return c

    lax.fori_loop(0, tiles, arrived, 0)

    def near(p, offs):
        def picked(h, n):
            v = src_s.at[lax.div(p, 4) * (ncell // 128) + n // 128, lax.rem(p, 4) * 2 + h, pl.ds(n % 128, 8)]
            return pick8(pool, lambda s: v[offs[s]], sub)

        his, los = [], []
        for n in range(0, ncell, 16):
            rows = [jnp.concatenate([picked(h, n), picked(h, n + 8)], axis=0) for h in range(2)]
            hi, lo = split(jnp.concatenate(rows, axis=1))
            his.append(hi)
            los.append(lo)
        w = near_w[p]
        both = nt(jnp.concatenate(his, axis=0), w)
        low = nt(jnp.concatenate(los, axis=0), w[0:128])
        acc[...] += both[:, 0:128] + both[:, 128:256] + low
        return offs

    lax.fori_loop(0, ops // 2, near, offs)

    lax.fori_loop(1, nplane, wait_all(plane_copy), 0)
    for i in range(nplane):
        boxes[i : i + 1, :] = plane[i]
    climb(line_levels, plane_levels, nplane, place)
    crossed = [dot3(sibs[...], cross_w[b, 0], cross_w[b, 1]) for b in range(2)]
    levels = line_levels + plane_levels
    row = lax.broadcasted_iota(jnp.int32, (16, 128), 0)
    bits = lax.rem(lax.shift_right_logical(jnp.full((16, 128), me, jnp.int32), row), 2)
    far[...] = jnp.where(bits == 0, crossed[0], crossed[1])
    g = jnp.zeros((8, 128), F32)
    for s in reversed(range(levels)):
        b = lax.rem(lax.shift_right_logical(me, s), 2)
        g = dot3(g, shift_w[b, 0], shift_w[b, 1]) + far[s : s + 1, :]
    spread = dot3(g, down_w[0], down_w[1])
    classes = jnp.concatenate([spread[0:1, o * 128 : (o + 1) * 128] for o in range(8)], axis=0)
    tiled = jnp.concatenate([classes] * 16, axis=0)
    for b in range(ncell // 128):
        block = (acc[b * 128 : (b + 1) * 128, :] + tiled).T
        out[:, b * 128 : (b + 1) * 128] = block[0:coef, :]


def shards(mesh, multipoles, sources, halo_cells, m2l_ops, cell_up, cell_down, side_ops):
    coef, ncell = multipoles.shape
    ops = sources.shape[0]
    nhalo = halo_cells.shape[1]
    ngx, ngy, ngz = (mesh.shape[a] for a in AXES)
    nplane = ngx * ngy
    hbm = pl.BlockSpec(memory_space=pl.ANY)
    vmem, dma = pltpu.VMEM, pltpu.SemaphoreType.DMA
    m2l = jnp.transpose(m2l_ops, (1, 0, 2)).reshape(coef * ops, coef)
    up = jnp.transpose(cell_up, (1, 0, 2)).reshape(coef * 8, coef)
    down = jnp.transpose(cell_down, (1, 0, 2)).reshape(coef * 8, coef)
    side = jnp.transpose(side_ops, (0, 2, 1, 3))
    return pl.pallas_call(
        functools.partial(kernel, (coef, ncell, ops, nhalo, ngx, ngy, ngz)),
        out_shape=jax.ShapeDtypeStruct((coef, ncell), F32),
        in_specs=[hbm] * 7,
        out_specs=pl.BlockSpec(memory_space=vmem),
        scratch_shapes=[
            vmem((coef, ncell), F32),
            vmem((ncell, 128), F32),
            vmem((ncell + 6 * nhalo, 128), F32),
            vmem((6, nhalo, 128), F32),
            pltpu.SMEM((ops // 8 * (ncell // 128), 8, 128), jnp.int32),
            pltpu.SMEM((6, nhalo), jnp.int32),
            vmem((coef * ops, coef), F32),
            vmem((coef * 8, coef), F32),
            vmem((coef * 8, coef), F32),
            vmem((3, coef, 2, coef), F32),
            vmem((ops // 2, 256, 256), BF16),
            vmem((2, 128, 1024), BF16),
            vmem((2, 1024, 128), BF16),
            vmem((2, 128, 256), BF16),
            vmem((2, 2, 128, 128), BF16),
            vmem((2, 2, 128, 128), BF16),
            vmem((ncell, 128), F32),
            vmem((2, 1, 128), F32),
            vmem((ngz, 1, 128), F32),
            vmem((nplane, 1, 128), F32),
            vmem((ngz, 128), F32),
            vmem((16, 128), F32),
            vmem((16, 128), F32),
            dma((6,)),
            dma((ops // 8 * (ncell // 128),)),
            dma((6,)),
            dma((6,)),
            dma((ngz,)),
            dma((ngz,)),
            dma((nplane,)),
            dma((nplane,)),
        ],
        compiler_params=pltpu.CompilerParams(
            collective_id=0, has_side_effects=True, vmem_limit_bytes=48 * 2**20
        ),
        cost_estimate=pl.CostEstimate(flops=3 * 10**9, bytes_accessed=4 * 10**6, transcendentals=0),
    )(multipoles, sources, halo_cells, m2l, up, down, side)


def solution(mesh):
    split_cells = P(None, AXES)
    split_rows = P(AXES, None)
    return jax.shard_map(
        functools.partial(shards, mesh),
        mesh=mesh,
        in_specs=(split_cells, split_rows, split_rows, P(), P(), P(), P()),
        out_specs=split_cells,
        check_vma=False,
    )
```

```python
import functools

import jax
import jax.numpy as jnp
from jax import lax
from jax.experimental import pallas as pl
from jax.experimental.pallas import tpu as pltpu
from jax.sharding import PartitionSpec as P

F32, BF16 = jnp.float32, jnp.bfloat16
MESH = pl.DeviceIdType.MESH
NT = (((1,), (1,)), ((), ()))
AXES = ("gx", "gy", "gz")
REACH = 4
LINE_STEP = 12


def split(x):
    hi = x.astype(BF16)
    return hi, (x - hi.astype(F32)).astype(BF16)


def nt(a, b):
    return lax.dot_general(a, b, NT, preferred_element_type=F32)


def dot3(x, wide, narrow):
    hi, lo = split(x)
    return nt(hi, wide) + (nt(lo, wide) + nt(hi, narrow))


def pick8(table, index_of, sub):
    block = None
    for s in range(8):
        row = jnp.broadcast_to(table[pl.ds(index_of(s), 1), :], (8, 128))
        block = row if block is None else jnp.where(sub == s, row, block)
    return block


def kernel(
    sizes, mult, sources, halo, m2l, up, down, side, out,
    cells, own, pool, faces, src_s, halo_s, m2l_v, up_v, down_v, side_v,
    near_w, up_w, down_w, merge_w, cross_w, shift_w, acc,
    mine, line, plane, boxes, sibs, far,
    in_sem, src_sem, known, face_send, face_recv, line_send, line_recv, plane_send, plane_recv,
):
    coef, ncell, ops, nhalo, ngx, ngy, ngz = sizes
    nplane = ngx * ngy
    gx, gy, gz = (lax.axis_index(a) for a in AXES)
    place = gx * ngy + gy
    me = place * ngz + gz
    zero = lax.shift_right_logical(me, 24)
    offs = tuple(zero + j for j in range(8))
    sub = lax.broadcasted_iota(jnp.int32, (8, 128), 0)

    loads = [
        pltpu.make_async_copy(mult, cells, in_sem.at[0]),
        pltpu.make_async_copy(halo, halo_s, in_sem.at[1]),
        pltpu.make_async_copy(up, up_v, in_sem.at[2]),
        pltpu.make_async_copy(side, side_v, in_sem.at[3]),
        pltpu.make_async_copy(m2l, m2l_v, in_sem.at[4]),
        pltpu.make_async_copy(down, down_v, in_sem.at[5]),
    ]
    loads[0].start()
    loads[1].start()

    def source_tile(t):
        g, q = lax.div(t, ncell // 128), lax.rem(t, ncell // 128)
        return pltpu.make_async_copy(
            sources.at[pl.ds(pl.multiple_of(g * 8, 8), 8), pl.ds(pl.multiple_of(q * 128, 128), 128)],
            src_s.at[t],
            src_sem.at[t],
        )

    tiles = ops // 8 * (ncell // 128)

    barrier = pltpu.get_barrier_semaphore()

    def in_line(j):
        return {"gz": lax.rem(gz + j, ngz)}

    def in_plane(j):
        other = lax.rem(place + j, nplane)
        return {"gx": lax.div(other, ngy), "gy": lax.rem(other, ngy)}

    def tell(semaphore, apart):
        @pl.when(gz + apart < ngz)
        def _():
            pl.semaphore_signal(semaphore, inc=1, device_id={"gz": gz + apart}, device_id_type=MESH)

        @pl.when(gz >= apart)
        def _():
            pl.semaphore_signal(semaphore, inc=1, device_id={"gz": gz - apart}, device_id_type=MESH)

    def greet(j, c):
        pl.semaphore_signal(barrier, inc=1, device_id=in_plane(j), device_id_type=MESH)
        return c

    for j in range(1, REACH + 1):
        tell(barrier, j)
    lax.fori_loop(1, nplane, greet, 0)
    greeted = jnp.minimum(gz, REACH) + jnp.minimum(ngz - 1 - gz, REACH) + nplane - 1

    rounds = max(0, (ngz // REACH).bit_length() - 1)

    def call(r):
        tell(known.at[r], REACH << r)

    def hear(r):
        apart = REACH << r
        pl.semaphore_wait(
            known.at[r], (gz >= apart).astype(jnp.int32) + (gz + apart < ngz).astype(jnp.int32)
        )

    loads[0].wait()
    for b in range(ncell // 128):
        block = jnp.concatenate(
            [cells[:, b * 128 : (b + 1) * 128], jnp.zeros((128 - coef, 128), F32)], axis=0
        ).T
        own[b * 128 : (b + 1) * 128, :] = block
        pool[b * 128 : (b + 1) * 128, :] = block

    for load in loads[2:]:
        load.start()
    loads[1].wait()
    neighbours = (
        (gx, ngx, lambda i: {"gx": i}),
        (gy, ngy, lambda i: {"gy": i}),
        (gz, ngz, lambda i: {"gz": i}),
    )

    def slot(i):
        return pool.at[pl.ds(ncell + i * nhalo, nhalo)]

    def face_copy(face, land, device):
        return pltpu.make_async_remote_copy(
            src_ref=faces.at[face],
            dst_ref=slot(land),
            send_sem=face_send.at[face],
            recv_sem=face_recv.at[land],
            device_id=device,
            device_id_type=MESH,
        )

    def gather_face(face):
        def part(i, c):
            for r in range(16):
                v = halo_s.at[face, pl.ds(i * 128 + r * 8, 8)]
                faces[face, pl.ds(pl.multiple_of(i * 128 + r * 8, 8), 8), :] = pick8(
                    own, lambda s: v[offs[s]], sub
                )
            return c

        lax.fori_loop(0, nhalo // 128, part, 0)

    for face in range(6):
        gather_face(face)
    pl.semaphore_wait(barrier, greeted)
    for a, (at, count, device) in enumerate(neighbours):
        @pl.when(at < count - 1)
        def _():
            face_copy(2 * a + 1, 2 * a, device(at + 1)).start()

        @pl.when(at > 0)
        def _():
            face_copy(2 * a, 2 * a + 1, device(at - 1)).start()

    call(0)

    def fetch(t, c):
        source_tile(t).start()
        return c

    lax.fori_loop(0, tiles, fetch, 0)

    for a, (at, count, _) in enumerate(neighbours):
        @pl.when(at == 0)
        def _():
            slot(2 * a)[...] = jnp.zeros((nhalo, 128), F32)

        @pl.when(at == count - 1)
        def _():
            slot(2 * a + 1)[...] = jnp.zeros((nhalo, 128), F32)

    for w in (up_w, down_w, merge_w, cross_w, shift_w, near_w):
        w[...] = jnp.zeros_like(w)
    loads[2].wait()
    for o in range(8):
        hi, lo = split(up_v[pl.ds(o, coef, 8), :])
        up_w[0, 0:coef, o * 128 : o * 128 + coef] = hi
        up_w[1, 0:coef, o * 128 : o * 128 + coef] = lo

    def add_class(i, total):
        for r in range(16):
            total = total + own[pl.ds(pl.multiple_of(i * 128 + r * 8, 8), 8), :]
        return total

    classes = lax.fori_loop(0, ncell // 128, add_class, jnp.zeros((8, 128), F32))
    flat = jnp.concatenate([classes[o : o + 1, :] for o in range(8)], axis=1)
    box = dot3(jnp.broadcast_to(flat, (8, 1024)), up_w[0], up_w[1])
    mine[0] = box[0:1, :]

    loads[3].wait()
    for b in range(2):
        for a, w in enumerate((merge_w, cross_w, shift_w)):
            hi, lo = split(side_v[a, :, b, :])
            if a == 0:
                w[0, 0:coef, b * 128 : b * 128 + coef] = hi
                w[1, 0:coef, b * 128 : b * 128 + coef] = lo
            else:
                w[b, 0, 0:coef, 0:coef] = hi
                w[b, 1, 0:coef, 0:coef] = lo
    loads[4].wait()

    def split_near(p, c):
        for h in range(2):
            hi, lo = split(m2l_v[pl.ds(p * 2 + h, coef, ops), :])
            near_w[p, 0:coef, h * 128 : h * 128 + coef] = hi
            near_w[p, 128 : 128 + coef, h * 128 : h * 128 + coef] = lo
        return c

    lax.fori_loop(0, ops // 2, split_near, 0)
    loads[5].wait()
    for o in range(8):
        hi, lo = split(down_v[pl.ds(o, coef, 8), :])
        down_w[0, o * 128 : o * 128 + coef, 0:coef] = hi
        down_w[1, o * 128 : o * 128 + coef, 0:coef] = lo
    acc[...] = jnp.zeros_like(acc)
    sibs[...] = jnp.zeros_like(sibs)

    def line_copy(j):
        return pltpu.make_async_remote_copy(
            src_ref=mine.at[0],
            dst_ref=line.at[gz],
            send_sem=line_send.at[j],
            recv_sem=line_recv.at[j],
            device_id=in_line(j),
            device_id_type=MESH,
        )

    def plane_copy(j):
        return pltpu.make_async_remote_copy(
            src_ref=mine.at[1],
            dst_ref=plane.at[place],
            send_sem=plane_send.at[j],
            recv_sem=plane_recv.at[j],
            device_id=in_plane(j),
            device_id_type=MESH,
        )

    def start_all(copy_of):
        def one(j, c):
            copy_of(j).start()
            return c

        return one

    def wait_all(copy_of):
        def one(j, c):
            copy_of(j).wait()
            return c

        return one

    line[gz] = box[0:1, :]

    def climb(first, sections, count, index):
        for s in range(sections):
            mask = lax.shift_right_logical(index, s)
            sib = mask + 1 - 2 * lax.rem(mask, 2)
            sibs[first + s : first + s + 1, :] = boxes[pl.ds(sib, 1), :]
            half = count >> (s + 1)
            if half:
                pairs = jnp.concatenate(
                    [boxes[pl.ds(0, half, 2), :], boxes[pl.ds(1, half, 2), :]], axis=1
                )
                boxes[0:half, :] = dot3(pairs, merge_w[0], merge_w[1])

    line_levels = ngz.bit_length() - 1
    plane_levels = nplane.bit_length() - 1

    def line_done():
        lax.fori_loop(1, ngz, wait_all(line_copy), 0)
        for i in range(ngz):
            boxes[i : i + 1, :] = line[i]
        climb(0, line_levels, ngz, gz)
        mine[1] = boxes[0:1, :]
        plane[place] = boxes[0:1, :]
        lax.fori_loop(1, nplane, start_all(plane_copy), 0)

    for a, (at, count, device) in enumerate(neighbours):
        @pl.when(at < count - 1)
        def _():
            face_copy(2 * a + 1, 2 * a, device(at + 1)).wait_send()
            face_copy(2 * a, 2 * a + 1, device(at + 1)).wait_recv()

        @pl.when(at > 0)
        def _():
            face_copy(2 * a, 2 * a + 1, device(at - 1)).wait_send()
            face_copy(2 * a + 1, 2 * a, device(at - 1)).wait_recv()

    def arrived(t, c):
        source_tile(t).wait()
        return c

    lax.fori_loop(0, tiles, arrived, 0)

    lead = jnp.maximum(ngz // 2 - gz, 0)

    def near(p, offs):
        @pl.when(p == 0)
        def _():
            hear(0)
            call(1)

        @pl.when(p == 1 + lax.div(jnp.minimum(lead, 12) * 5, 12))
        def _():
            hear(1)
            call(2)

        @pl.when(p == 2 + lax.div(lead, 2))
        def _():
            hear(2)
            lax.fori_loop(1, ngz, start_all(line_copy), 0)

        pl.when(p == LINE_STEP)(line_done)

        def picked(h, n):
            v = src_s.at[lax.div(p, 4) * (ncell // 128) + n // 128, lax.rem(p, 4) * 2 + h, pl.ds(n % 128, 8)]
            return pick8(pool, lambda s: v[offs[s]], sub)

        his, los = [], []
        for n in range(0, ncell, 16):
            rows = [jnp.concatenate([picked(h, n), picked(h, n + 8)], axis=0) for h in range(2)]
            hi, lo = split(jnp.concatenate(rows, axis=1))
            his.append(hi)
            los.append(lo)
        w = near_w[p]
        both = nt(jnp.concatenate(his, axis=0), w)
        low = nt(jnp.concatenate(los, axis=0), w[0:128])
        acc[...] += both[:, 0:128] + both[:, 128:256] + low
        return offs

    lax.fori_loop(0, ops // 2, near, offs)

    lax.fori_loop(1, nplane, wait_all(plane_copy), 0)
    for i in range(nplane):
        boxes[i : i + 1, :] = plane[i]
    climb(line_levels, plane_levels, nplane, place)
    crossed = [dot3(sibs[...], cross_w[b, 0], cross_w[b, 1]) for b in range(2)]
    levels = line_levels + plane_levels
    row = lax.broadcasted_iota(jnp.int32, (16, 128), 0)
    bits = lax.rem(lax.shift_right_logical(jnp.full((16, 128), me, jnp.int32), row), 2)
    far[...] = jnp.where(bits == 0, crossed[0], crossed[1])
    g = jnp.zeros((8, 128), F32)
    for s in reversed(range(levels)):
        b = lax.rem(lax.shift_right_logical(me, s), 2)
        g = dot3(g, shift_w[b, 0], shift_w[b, 1]) + far[s : s + 1, :]
    spread = dot3(g, down_w[0], down_w[1])
    classes = jnp.concatenate([spread[0:1, o * 128 : (o + 1) * 128] for o in range(8)], axis=0)
    spread = jnp.concatenate([classes] * 16, axis=0).T
    for b in range(ncell // 128):
        block = acc[b * 128 : (b + 1) * 128, :].T + spread
        out[:, b * 128 : (b + 1) * 128] = block[0:coef, :]


def shards(mesh, multipoles, sources, halo_cells, m2l_ops, cell_up, cell_down, side_ops):
    coef, ncell = multipoles.shape
    ops = sources.shape[0]
    nhalo = halo_cells.shape[1]
    ngx, ngy, ngz = (mesh.shape[a] for a in AXES)
    nplane = ngx * ngy
    hbm = pl.BlockSpec(memory_space=pltpu.HBM)
    vmem, dma = pltpu.VMEM, pltpu.SemaphoreType.DMA
    m2l = jnp.transpose(m2l_ops, (1, 0, 2)).reshape(coef * ops, coef)
    up = jnp.transpose(cell_up, (1, 0, 2)).reshape(coef * 8, coef)
    down = jnp.transpose(cell_down, (1, 0, 2)).reshape(coef * 8, coef)
    side = jnp.transpose(side_ops, (0, 2, 1, 3))
    return pl.pallas_call(
        functools.partial(kernel, (coef, ncell, ops, nhalo, ngx, ngy, ngz)),
        out_shape=jax.ShapeDtypeStruct((coef, ncell), F32),
        in_specs=[hbm] * 7,
        out_specs=pl.BlockSpec(memory_space=vmem),
        scratch_shapes=[
            vmem((coef, ncell), F32),
            vmem((ncell, 128), F32),
            vmem((ncell + 6 * nhalo, 128), F32),
            vmem((6, nhalo, 128), F32),
            pltpu.SMEM((ops // 8 * (ncell // 128), 8, 128), jnp.int32),
            pltpu.SMEM((6, nhalo), jnp.int32),
            vmem((coef * ops, coef), F32),
            vmem((coef * 8, coef), F32),
            vmem((coef * 8, coef), F32),
            vmem((3, coef, 2, coef), F32),
            vmem((ops // 2, 256, 256), BF16),
            vmem((2, 128, 1024), BF16),
            vmem((2, 1024, 128), BF16),
            vmem((2, 128, 256), BF16),
            vmem((2, 2, 128, 128), BF16),
            vmem((2, 2, 128, 128), BF16),
            vmem((ncell, 128), F32),
            vmem((2, 1, 128), F32),
            vmem((ngz, 1, 128), F32),
            vmem((nplane, 1, 128), F32),
            vmem((ngz, 128), F32),
            vmem((16, 128), F32),
            vmem((16, 128), F32),
            dma((6,)),
            dma((ops // 8 * (ncell // 128),)),
            pltpu.SemaphoreType.REGULAR((4,)),
            dma((6,)),
            dma((6,)),
            dma((ngz,)),
            dma((ngz,)),
            dma((nplane,)),
            dma((nplane,)),
        ],
        compiler_params=pltpu.CompilerParams(
            collective_id=0, has_side_effects=True, vmem_limit_bytes=63 * 2**20
        ),
        cost_estimate=pl.CostEstimate(flops=3 * 10**9, bytes_accessed=4 * 10**6, transcendentals=0),
    )(multipoles, sources, halo_cells, m2l, up, down, side)


def solution(mesh):
    split_cells = P(None, AXES)
    split_rows = P(AXES, None)
    return jax.shard_map(
        functools.partial(shards, mesh),
        mesh=mesh,
        in_specs=(split_cells, split_rows, split_rows, P(), P(), P(), P()),
        out_specs=split_cells,
        check_vma=False,
    )
```

```python
import functools

import jax
import jax.numpy as jnp
from jax import lax
from jax.experimental import pallas as pl
from jax.experimental.pallas import tpu as pltpu
from jax.sharding import PartitionSpec as P

F32, BF16 = jnp.float32, jnp.bfloat16
MESH = pl.DeviceIdType.MESH
NT = (((1,), (1,)), ((), ()))
AXES = ("gx", "gy", "gz")
UP_STEP = 9
LINE_STEP = 12


def split(x):
    hi = x.astype(BF16)
    return hi, (x - hi.astype(F32)).astype(BF16)


def nt(a, b):
    return lax.dot_general(a, b, NT, preferred_element_type=F32)


def dot3(x, wide, narrow):
    hi, lo = split(x)
    return nt(hi, wide) + (nt(lo, wide) + nt(hi, narrow))


def nn3(a, b):
    ah, al = split(a)
    bh, bl = split(b)
    dot = functools.partial(jnp.dot, preferred_element_type=F32)
    return dot(ah, bh) + (dot(al, bh) + dot(ah, bl))


def pick8(table, index_of, sub):
    block = None
    for s in range(8):
        row = jnp.broadcast_to(table[pl.ds(index_of(s), 1), :], (8, 128))
        block = row if block is None else jnp.where(sub == s, row, block)
    return block


def kernel(
    sizes, mult, sources, halo, m2l, up, down, side, out,
    cells, own, pool, faces, src_s, halo_s, m2l_v, up_v, down_v, side_v,
    near_w, up_w, down_w, side_w, merge_w, merge4_w, far_w, acc,
    mine, line, plane, boxes, sibs,
    in_sem, src_sem, face_send, face_recv, line_send, line_recv, plane_send, plane_recv,
):
    coef, ncell, ops, nhalo, ngx, ngy, ngz = sizes
    nplane = ngx * ngy
    gx, gy, gz = (lax.axis_index(a) for a in AXES)
    place = gx * ngy + gy
    me = place * ngz + gz
    zero = lax.shift_right_logical(me, 24)
    offs = tuple(zero + j for j in range(8))
    sub = lax.broadcasted_iota(jnp.int32, (8, 128), 0)

    loads = [
        pltpu.make_async_copy(mult, cells, in_sem.at[0]),
        pltpu.make_async_copy(halo, halo_s, in_sem.at[1]),
        pltpu.make_async_copy(up, up_v, in_sem.at[2]),
        pltpu.make_async_copy(side, side_v, in_sem.at[3]),
        pltpu.make_async_copy(m2l, m2l_v, in_sem.at[4]),
        pltpu.make_async_copy(down, down_v, in_sem.at[5]),
    ]
    loads[0].start()
    loads[1].start()

    def source_tile(t):
        g, q = lax.div(t, ncell // 128), lax.rem(t, ncell // 128)
        return pltpu.make_async_copy(
            sources.at[pl.ds(pl.multiple_of(g * 8, 8), 8), pl.ds(pl.multiple_of(q * 128, 128), 128)],
            src_s.at[t],
            src_sem.at[0],
        )

    tiles = ops // 8 * (ncell // 128)

    barrier = pltpu.get_barrier_semaphore()

    def in_plane(j):
        other = lax.rem(place + j, nplane)
        return {"gx": lax.div(other, ngy), "gy": lax.rem(other, ngy)}

    def greet(device):
        pl.semaphore_signal(barrier, inc=1, device_id=device, device_id_type=MESH)

    def greet_plane(j, c):
        greet(in_plane(j))
        return c

    def greet_up(i, c):
        greet({"gz": i})
        return c

    pl.when(gz > 0)(lambda: greet({"gz": gz - 1}))
    lax.fori_loop(gz + 1, ngz, greet_up, 0)
    lax.fori_loop(1, nplane, greet_plane, 0)
    greeted = nplane - 1 + gz + (gz < ngz - 1).astype(jnp.int32)

    loads[0].wait()
    for b in range(ncell // 128):
        block = jnp.concatenate(
            [cells[:, b * 128 : (b + 1) * 128], jnp.zeros((128 - coef, 128), F32)], axis=0
        ).T
        own[b * 128 : (b + 1) * 128, :] = block
        pool[b * 128 : (b + 1) * 128, :] = block

    for load in loads[2:]:
        load.start()
    loads[1].wait()
    neighbours = (
        (gx, ngx, lambda i: {"gx": i}),
        (gy, ngy, lambda i: {"gy": i}),
        (gz, ngz, lambda i: {"gz": i}),
    )

    def slot(i):
        return pool.at[pl.ds(ncell + i * nhalo, nhalo)]

    def face_copy(face, land, device):
        return pltpu.make_async_remote_copy(
            src_ref=faces.at[face],
            dst_ref=slot(land),
            send_sem=face_send.at[face],
            recv_sem=face_recv.at[land],
            device_id=device,
            device_id_type=MESH,
        )

    def gather_face(face):
        def part(i, c):
            for r in range(16):
                v = halo_s.at[face, pl.ds(i * 128 + r * 8, 8)]
                faces[face, pl.ds(pl.multiple_of(i * 128 + r * 8, 8), 8), :] = pick8(
                    own, lambda s: v[offs[s]], sub
                )
            return c

        lax.fori_loop(0, nhalo // 128, part, 0)

    for a, (at, count, device) in enumerate(neighbours):
        gather_face(2 * a)
        gather_face(2 * a + 1)
        if a == 0:
            pl.semaphore_wait(barrier, greeted)

        @pl.when(at < count - 1)
        def _():
            face_copy(2 * a + 1, 2 * a, device(at + 1)).start()

        @pl.when(at > 0)
        def _():
            face_copy(2 * a, 2 * a + 1, device(at - 1)).start()

    def fetch(t, c):
        source_tile(t).start()
        return c

    lax.fori_loop(0, tiles, fetch, 0)

    for a, (at, count, _) in enumerate(neighbours):
        @pl.when(at == 0)
        def _():
            slot(2 * a)[...] = jnp.zeros((nhalo, 128), F32)

        @pl.when(at == count - 1)
        def _():
            slot(2 * a + 1)[...] = jnp.zeros((nhalo, 128), F32)

    for w in (up_w, down_w, side_w, near_w):
        w[...] = jnp.zeros_like(w)
    loads[2].wait()
    for o in range(8):
        hi, lo = split(up_v[pl.ds(o, coef, 8), :])
        up_w[0, 0:coef, o * 128 : o * 128 + coef] = hi
        up_w[1, 0:coef, o * 128 : o * 128 + coef] = lo

    def add_class(i, total):
        for r in range(16):
            total = total + own[pl.ds(pl.multiple_of(i * 128 + r * 8, 8), 8), :]
        return total

    classes = lax.fori_loop(0, ncell // 128, add_class, jnp.zeros((8, 128), F32))
    flat = jnp.concatenate([classes[o : o + 1, :] for o in range(8)], axis=1)
    box = dot3(jnp.broadcast_to(flat, (8, 1024)), up_w[0], up_w[1])
    mine[0] = box[0:1, :]

    loads[3].wait()
    for a in range(3):
        for b in range(2):
            side_w[a, b, 0:coef, 0:coef] = side_v[a, :, b, :]
    merge = jnp.concatenate([side_w[0, 0], side_w[0, 1]], axis=1)
    merge_w[0], merge_w[1] = split(merge)
    four = nn3(jnp.concatenate([side_w[0, 0], side_w[0, 1]], axis=0), merge)
    merge4_w[0], merge4_w[1] = split(jnp.concatenate([four[0:128], four[128:256]], axis=1))
    levels = (ngz * nplane).bit_length() - 1
    turn = [lax.rem(lax.shift_right_logical(me, s), 2) for s in range(levels)]
    step = [side_w[2, turn[s]] for s in range(levels)]
    two = [nn3(step[s], step[s + 1]) for s in range(0, levels - 1, 2)]
    third = nn3(two[0], jnp.concatenate([step[2], two[1]], axis=1))
    rest = nn3(two[2], jnp.concatenate([step[6], two[3]], axis=1))
    upper = nn3(third[:, 128:256], jnp.concatenate([step[4], two[2], rest], axis=1))
    way = [None, step[0], two[0], third[:, 0:128], third[:, 128:256]]
    way += [upper[:, i * 128 : (i + 1) * 128] for i in range(4)]
    for s in range(levels):
        cross = side_w[1, turn[s]]
        far_w[0, :, s * 128 : (s + 1) * 128], far_w[1, :, s * 128 : (s + 1) * 128] = split(
            nn3(way[s], cross) if s else cross
        )
    loads[5].wait()
    for o in range(8):
        hi, lo = split(down_v[pl.ds(o, coef, 8), :])
        down_w[0, o * 128 : o * 128 + coef, 0:coef] = hi
        down_w[1, o * 128 : o * 128 + coef, 0:coef] = lo
    acc[...] = jnp.zeros_like(acc)
    sibs[...] = jnp.zeros_like(sibs)

    def line_copy(sender, device):
        return pltpu.make_async_remote_copy(
            src_ref=mine.at[0],
            dst_ref=line.at[sender],
            send_sem=line_send.at[0],
            recv_sem=line_recv.at[sender],
            device_id={"gz": device},
            device_id_type=MESH,
        )

    def send_box(to, c):
        line_copy(gz, to).start()
        return c

    def get_box(sender, c):
        line_copy(sender, sender).wait_recv()
        return c

    def plane_copy(j):
        return pltpu.make_async_remote_copy(
            src_ref=mine.at[1],
            dst_ref=plane.at[place],
            send_sem=plane_send.at[0],
            recv_sem=plane_recv.at[0],
            device_id=in_plane(j),
            device_id_type=MESH,
        )

    def send_top(j, c):
        plane_copy(j).start()
        return c

    def all_of(buffer, count, send, recv):
        every = buffer.at[pl.ds(0, count - 1)]
        return pltpu.make_async_remote_copy(
            src_ref=every,
            dst_ref=every,
            send_sem=send.at[0],
            recv_sem=recv.at[0],
            device_id=in_plane(1),
            device_id_type=MESH,
        )

    lax.fori_loop(0, gz, send_box, 0)
    line[gz] = box[0:1, :]

    def quads(count):
        rows = [boxes[pl.ds(i, count // 4, 4), :] for i in range(4)]
        return dot3(jnp.concatenate(rows, axis=1), merge4_w[0], merge4_w[1])

    def pair(index):
        return jnp.concatenate([boxes[pl.ds(2 * index, 1), :], boxes[pl.ds(2 * index + 1, 1), :]], axis=1)

    def merged(rows):
        return dot3(jnp.concatenate(rows, axis=0), merge_w[0], merge_w[1])

    def sibling(index, s):
        mask = lax.shift_right_logical(index, s)
        return mask + 1 - 2 * lax.rem(mask, 2)

    def line_done():
        lax.fori_loop(0, gz, get_box, 0)
        for i in range(ngz):
            boxes[i : i + 1, :] = line[i]
        sibs[0:1, :] = boxes[pl.ds(sibling(gz, 0), 1), :]
        first = pair(sibling(gz, 1))
        boxes[0:8, :] = quads(32)
        sibs[2:3, :] = boxes[pl.ds(sibling(gz, 2), 1), :]
        third = pair(sibling(gz, 3))
        boxes[0:2, :] = quads(8)
        sibs[4:5, :] = boxes[pl.ds(sibling(gz, 4), 1), :]
        top = merged([first, third, pair(0)])
        sibs[1:2, :] = top[0:1, :]
        sibs[3:4, :] = top[1:2, :]
        mine[1] = top[2:3, :]
        plane[place] = top[2:3, :]
        lax.fori_loop(1, nplane, send_top, 0)

    for a, (at, count, device) in enumerate(neighbours):
        @pl.when(at < count - 1)
        def _():
            face_copy(2 * a + 1, 2 * a, device(at + 1)).wait_send()
            face_copy(2 * a, 2 * a + 1, device(at + 1)).wait_recv()

        @pl.when(at > 0)
        def _():
            face_copy(2 * a, 2 * a + 1, device(at - 1)).wait_send()
            face_copy(2 * a + 1, 2 * a, device(at - 1)).wait_recv()

    pltpu.make_async_copy(src_s, src_s, src_sem.at[0]).wait()

    def split_near(p, to):
        for h in range(2):
            hi, lo = split(m2l_v[pl.ds(p * 2 + h, coef, ops), :])
            near_w[to, 0:coef, h * 128 : h * 128 + coef] = hi
            near_w[to, 128 : 128 + coef, h * 128 : h * 128 + coef] = lo

    loads[4].wait()
    split_near(0, 0)

    def near(p, offs):
        @pl.when(p == UP_STEP)
        def _():
            lax.fori_loop(gz + 1, ngz, get_box, 0)
            lax.fori_loop(gz + 1, ngz, send_box, 0)

        pl.when(p == LINE_STEP)(line_done)

        def picked(h, n):
            v = src_s.at[lax.div(p, 4) * (ncell // 128) + n // 128, lax.rem(p, 4) * 2 + h, pl.ds(n % 128, 8)]
            return pick8(pool, lambda s: v[offs[s]], sub)

        now = lax.rem(p, 2)
        his, los = [], []
        for n in range(0, ncell, 16):
            rows = [jnp.concatenate([picked(h, n), picked(h, n + 8)], axis=0) for h in range(2)]
            hi, lo = split(jnp.concatenate(rows, axis=1))
            his.append(hi)
            los.append(lo)
        w = near_w[now]
        both = nt(jnp.concatenate(his, axis=0), w)
        low = nt(jnp.concatenate(los, axis=0), w[0:128])
        acc[...] += both[:, 0:128] + both[:, 128:256] + low
        split_near(jnp.minimum(p + 1, ops // 2 - 1), 1 - now)
        return offs

    lax.fori_loop(0, ops // 2, near, offs)

    all_of(plane, nplane, plane_send, plane_recv).wait()
    all_of(line, ngz, line_send, line_recv).wait_send()
    for i in range(nplane):
        boxes[i : i + 1, :] = plane[i]
    known_sibs = [sibs[s : s + 1, :] for s in range(5)]
    known_sibs.append(boxes[pl.ds(sibling(place, 0), 1), :])
    sixth = pair(sibling(place, 1))
    boxes[0:4, :] = quads(16)
    known_sibs.append(None)
    known_sibs.append(boxes[pl.ds(sibling(place, 2), 1), :])
    last = merged([sixth, pair(sibling(place, 3))])
    known_sibs[6] = last[0:1, :]
    known_sibs.append(last[1:2, :])
    every = jnp.concatenate(known_sibs, axis=1)
    g = dot3(every, far_w[0, :, 0 : levels * 128], far_w[1, :, 0 : levels * 128])
    spread = dot3(g, down_w[0], down_w[1])
    classes = jnp.concatenate([spread[0:1, o * 128 : (o + 1) * 128] for o in range(8)], axis=0)
    spread = jnp.concatenate([classes] * 16, axis=0).T
    for b in range(ncell // 128):
        block = acc[b * 128 : (b + 1) * 128, :].T + spread
        out[:, b * 128 : (b + 1) * 128] = block[0:coef, :]


def shards(mesh, multipoles, sources, halo_cells, m2l_ops, cell_up, cell_down, side_ops):
    coef, ncell = multipoles.shape
    ops = sources.shape[0]
    nhalo = halo_cells.shape[1]
    ngx, ngy, ngz = (mesh.shape[a] for a in AXES)
    nplane = ngx * ngy
    hbm = pl.BlockSpec(memory_space=pltpu.HBM)
    vmem, dma = pltpu.VMEM, pltpu.SemaphoreType.DMA
    m2l = jnp.transpose(m2l_ops, (1, 0, 2)).reshape(coef * ops, coef)
    up = jnp.transpose(cell_up, (1, 0, 2)).reshape(coef * 8, coef)
    down = jnp.transpose(cell_down, (1, 0, 2)).reshape(coef * 8, coef)
    side = jnp.transpose(side_ops, (0, 2, 1, 3))
    return pl.pallas_call(
        functools.partial(kernel, (coef, ncell, ops, nhalo, ngx, ngy, ngz)),
        out_shape=jax.ShapeDtypeStruct((coef, ncell), F32),
        in_specs=[hbm] * 7,
        out_specs=pl.BlockSpec(memory_space=vmem),
        scratch_shapes=[
            vmem((coef, ncell), F32),
            vmem((ncell, 128), F32),
            vmem((ncell + 6 * nhalo, 128), F32),
            vmem((6, nhalo, 128), F32),
            pltpu.SMEM((ops // 8 * (ncell // 128), 8, 128), jnp.int32),
            pltpu.SMEM((6, nhalo), jnp.int32),
            vmem((coef * ops, coef), F32),
            vmem((coef * 8, coef), F32),
            vmem((coef * 8, coef), F32),
            vmem((3, coef, 2, coef), F32),
            vmem((2, 256, 256), BF16),
            vmem((2, 128, 1024), BF16),
            vmem((2, 1024, 128), BF16),
            vmem((3, 2, 128, 128), F32),
            vmem((2, 128, 256), BF16),
            vmem((2, 128, 512), BF16),
            vmem((2, 128, 128 * 16), BF16),
            vmem((ncell, 128), F32),
            vmem((2, 1, 128), F32),
            vmem((ngz, 1, 128), F32),
            vmem((nplane, 1, 128), F32),
            vmem((ngz, 128), F32),
            vmem((16, 128), F32),
            dma((6,)),
            dma((1,)),
            dma((6,)),
            dma((6,)),
            dma((1,)),
            dma((ngz,)),
            dma((1,)),
            dma((1,)),
        ],
        compiler_params=pltpu.CompilerParams(
            collective_id=0, has_side_effects=True, vmem_limit_bytes=63 * 2**20
        ),
        cost_estimate=pl.CostEstimate(flops=3 * 10**9, bytes_accessed=4 * 10**6, transcendentals=0),
    )(multipoles, sources, halo_cells, m2l, up, down, side)


def solution(mesh):
    split_cells = P(None, AXES)
    split_rows = P(AXES, None)
    return jax.shard_map(
        functools.partial(shards, mesh),
        mesh=mesh,
        in_specs=(split_cells, split_rows, split_rows, P(), P(), P(), P()),
        out_specs=split_cells,
        check_vma=False,
    )
```

```python
import functools

import jax
import jax.numpy as jnp
from jax import lax
from jax.experimental import pallas as pl
from jax.experimental.pallas import tpu as pltpu
from jax.sharding import PartitionSpec as P

F32, BF16 = jnp.float32, jnp.bfloat16
MESH = pl.DeviceIdType.MESH
NT = (((1,), (1,)), ((), ()))
AXES = ("gx", "gy", "gz")
UP_STEP = 9
LINE_STEP = 13


def split(x):
    hi = x.astype(BF16)
    return hi, (x - hi.astype(F32)).astype(BF16)


def nt(a, b):
    return lax.dot_general(a, b, NT, preferred_element_type=F32)


def dot3(x, wide, narrow):
    hi, lo = split(x)
    return nt(hi, wide) + (nt(lo, wide) + nt(hi, narrow))


def nn3(a, b):
    ah, al = split(a)
    bh, bl = split(b)
    dot = functools.partial(jnp.dot, preferred_element_type=F32)
    return dot(ah, bh) + (dot(al, bh) + dot(ah, bl))


def pick8(table, index_of, sub):
    block = None
    for s in range(8):
        row = jnp.broadcast_to(table[pl.ds(index_of(s), 1), :], (8, 128))
        block = row if block is None else jnp.where(sub == s, row, block)
    return block


def kernel(
    sizes, mult, sources, halo, m2l, up, down, side, out,
    cells, own, pool, faces, src_s, halo_s, m2l_v, up_v, down_v, side_v,
    near_w, up_w, down_w, side_w, merge_w, merge4_w, far_w, acc,
    mine, line, plane, boxes, sibs,
    in_sem, src_sem, face_send, face_recv, line_send, line_recv, plane_send, plane_recv,
):
    coef, ncell, ops, nhalo, ngx, ngy, ngz = sizes
    nplane = ngx * ngy
    gx, gy, gz = (lax.axis_index(a) for a in AXES)
    place = gx * ngy + gy
    me = place * ngz + gz
    zero = lax.shift_right_logical(me, 24)
    offs = tuple(zero + j for j in range(8))
    sub = lax.broadcasted_iota(jnp.int32, (8, 128), 0)

    loads = [
        pltpu.make_async_copy(mult, cells, in_sem.at[0]),
        pltpu.make_async_copy(halo, halo_s, in_sem.at[1]),
        pltpu.make_async_copy(side, side_v, in_sem.at[3]),
    ]
    loads[0].start()
    loads[1].start()

    def slices(table, to, sem):
        def one(k, c):
            pltpu.make_async_copy(table.at[:, k, :], to.at[k], in_sem.at[sem]).start()
            return c

        lax.fori_loop(0, to.shape[0], one, 0)

    def arrive(to, sem):
        pltpu.make_async_copy(to, to, in_sem.at[sem]).wait()

    def source_tile(t):
        g, q = lax.div(t, ncell // 128), lax.rem(t, ncell // 128)
        return pltpu.make_async_copy(
            sources.at[pl.ds(pl.multiple_of(g * 8, 8), 8), pl.ds(pl.multiple_of(q * 128, 128), 128)],
            src_s.at[t],
            src_sem.at[0],
        )

    tiles = ops // 8 * (ncell // 128)

    barrier = pltpu.get_barrier_semaphore()

    def in_plane(j):
        other = lax.rem(place + j, nplane)
        return {"gx": lax.div(other, ngy), "gy": lax.rem(other, ngy)}

    def greet(device):
        pl.semaphore_signal(barrier, inc=1, device_id=device, device_id_type=MESH)

    def greet_plane(j, c):
        greet(in_plane(j))
        return c

    def greet_up(i, c):
        greet({"gz": i})
        return c

    pl.when(gz > 0)(lambda: greet({"gz": gz - 1}))
    lax.fori_loop(gz + 1, ngz, greet_up, 0)
    lax.fori_loop(1, nplane, greet_plane, 0)
    greeted = nplane - 1 + gz + (gz < ngz - 1).astype(jnp.int32)

    loads[0].wait()
    for b in range(ncell // 128):
        block = jnp.concatenate(
            [cells[:, b * 128 : (b + 1) * 128], jnp.zeros((128 - coef, 128), F32)], axis=0
        ).T
        own[b * 128 : (b + 1) * 128, :] = block
        pool[b * 128 : (b + 1) * 128, :] = block

    slices(up, up_v, 2)
    loads[2].start()
    slices(down, down_v, 5)
    slices(m2l, m2l_v, 4)
    loads[1].wait()
    neighbours = (
        (gx, ngx, lambda i: {"gx": i}),
        (gy, ngy, lambda i: {"gy": i}),
        (gz, ngz, lambda i: {"gz": i}),
    )

    def slot(i):
        return pool.at[pl.ds(ncell + i * nhalo, nhalo)]

    def face_copy(face, land, device):
        return pltpu.make_async_remote_copy(
            src_ref=faces.at[face],
            dst_ref=slot(land),
            send_sem=face_send.at[face],
            recv_sem=face_recv.at[land],
            device_id=device,
            device_id_type=MESH,
        )

    def gather_face(face):
        def part(i, c):
            for r in range(16):
                v = halo_s.at[face, pl.ds(i * 128 + r * 8, 8)]
                faces[face, pl.ds(pl.multiple_of(i * 128 + r * 8, 8), 8), :] = pick8(
                    own, lambda s: v[offs[s]], sub
                )
            return c

        lax.fori_loop(0, nhalo // 128, part, 0)

    for a, (at, count, device) in enumerate(neighbours):
        gather_face(2 * a)
        gather_face(2 * a + 1)
        if a == 0:
            pl.semaphore_wait(barrier, greeted)

        @pl.when(at < count - 1)
        def _():
            face_copy(2 * a + 1, 2 * a, device(at + 1)).start()

        @pl.when(at > 0)
        def _():
            face_copy(2 * a, 2 * a + 1, device(at - 1)).start()

    def fetch(t, c):
        source_tile(t).start()
        return c

    lax.fori_loop(0, tiles, fetch, 0)

    for a, (at, count, _) in enumerate(neighbours):
        @pl.when(at == 0)
        def _():
            slot(2 * a)[...] = jnp.zeros((nhalo, 128), F32)

        @pl.when(at == count - 1)
        def _():
            slot(2 * a + 1)[...] = jnp.zeros((nhalo, 128), F32)

    for w in (up_w, down_w, side_w, near_w):
        w[...] = jnp.zeros_like(w)
    arrive(up_v, 2)
    for o in range(8):
        hi, lo = split(up_v[o])
        up_w[0, 0:coef, o * 128 : o * 128 + coef] = hi
        up_w[1, 0:coef, o * 128 : o * 128 + coef] = lo

    def add_class(i, total):
        for r in range(16):
            total = total + own[pl.ds(pl.multiple_of(i * 128 + r * 8, 8), 8), :]
        return total

    classes = lax.fori_loop(0, ncell // 128, add_class, jnp.zeros((8, 128), F32))
    flat = jnp.concatenate([classes[o : o + 1, :] for o in range(8)], axis=1)
    box = dot3(jnp.broadcast_to(flat, (8, 1024)), up_w[0], up_w[1])
    mine[0] = box[0:1, :]

    loads[2].wait()
    for a in range(3):
        for b in range(2):
            side_w[a, b, 0:coef, 0:coef] = side_v[a, :, b, :]
    merge = jnp.concatenate([side_w[0, 0], side_w[0, 1]], axis=1)
    merge_w[0], merge_w[1] = split(merge)
    four = nn3(jnp.concatenate([side_w[0, 0], side_w[0, 1]], axis=0), merge)
    merge4_w[0], merge4_w[1] = split(jnp.concatenate([four[0:128], four[128:256]], axis=1))
    levels = (ngz * nplane).bit_length() - 1
    turn = [lax.rem(lax.shift_right_logical(me, s), 2) for s in range(levels)]
    step = [side_w[2, turn[s]] for s in range(levels)]
    two = [nn3(step[s], step[s + 1]) for s in range(0, levels - 1, 2)]
    third = nn3(two[0], jnp.concatenate([step[2], two[1]], axis=1))
    rest = nn3(two[2], jnp.concatenate([step[6], two[3]], axis=1))
    upper = nn3(third[:, 128:256], jnp.concatenate([step[4], two[2], rest], axis=1))
    way = [None, step[0], two[0], third[:, 0:128], third[:, 128:256]]
    way += [upper[:, i * 128 : (i + 1) * 128] for i in range(4)]
    for s in range(levels):
        cross = side_w[1, turn[s]]
        far_w[0, :, s * 128 : (s + 1) * 128], far_w[1, :, s * 128 : (s + 1) * 128] = split(
            nn3(way[s], cross) if s else cross
        )
    arrive(down_v, 5)
    for o in range(8):
        hi, lo = split(down_v[o])
        down_w[0, o * 128 : o * 128 + coef, 0:coef] = hi
        down_w[1, o * 128 : o * 128 + coef, 0:coef] = lo
    acc[...] = jnp.zeros_like(acc)
    sibs[...] = jnp.zeros_like(sibs)

    def line_copy(sender, device):
        return pltpu.make_async_remote_copy(
            src_ref=mine.at[0],
            dst_ref=line.at[sender],
            send_sem=line_send.at[0],
            recv_sem=line_recv.at[sender],
            device_id={"gz": device},
            device_id_type=MESH,
        )

    def send_box(to, c):
        line_copy(gz, to).start()
        return c

    def get_box(sender, c):
        line_copy(sender, sender).wait_recv()
        return c

    def plane_copy(j):
        return pltpu.make_async_remote_copy(
            src_ref=mine.at[1],
            dst_ref=plane.at[place],
            send_sem=plane_send.at[0],
            recv_sem=plane_recv.at[0],
            device_id=in_plane(j),
            device_id_type=MESH,
        )

    def send_top(j, c):
        plane_copy(j).start()
        return c

    def all_of(buffer, count, send, recv):
        every = buffer.at[pl.ds(0, count - 1)]
        return pltpu.make_async_remote_copy(
            src_ref=every,
            dst_ref=every,
            send_sem=send.at[0],
            recv_sem=recv.at[0],
            device_id=in_plane(1),
            device_id_type=MESH,
        )

    lax.fori_loop(0, gz, send_box, 0)
    line[gz] = box[0:1, :]

    def quads(count):
        rows = [boxes[pl.ds(i, count // 4, 4), :] for i in range(4)]
        return dot3(jnp.concatenate(rows, axis=1), merge4_w[0], merge4_w[1])

    def pair(index):
        return jnp.concatenate([boxes[pl.ds(2 * index, 1), :], boxes[pl.ds(2 * index + 1, 1), :]], axis=1)

    def merged(rows):
        return dot3(jnp.concatenate(rows, axis=0), merge_w[0], merge_w[1])

    def sibling(index, s):
        mask = lax.shift_right_logical(index, s)
        return mask + 1 - 2 * lax.rem(mask, 2)

    def line_done():
        lax.fori_loop(0, gz, get_box, 0)
        for i in range(ngz):
            boxes[i : i + 1, :] = line[i]
        sibs[0:1, :] = boxes[pl.ds(sibling(gz, 0), 1), :]
        first = pair(sibling(gz, 1))
        boxes[0:8, :] = quads(32)
        sibs[2:3, :] = boxes[pl.ds(sibling(gz, 2), 1), :]
        third = pair(sibling(gz, 3))
        boxes[0:2, :] = quads(8)
        sibs[4:5, :] = boxes[pl.ds(sibling(gz, 4), 1), :]
        top = merged([first, third, pair(0)])
        sibs[1:2, :] = top[0:1, :]
        sibs[3:4, :] = top[1:2, :]
        mine[1] = top[2:3, :]
        plane[place] = top[2:3, :]
        lax.fori_loop(1, nplane, send_top, 0)

    for a, (at, count, device) in enumerate(neighbours):
        @pl.when(at < count - 1)
        def _():
            face_copy(2 * a + 1, 2 * a, device(at + 1)).wait_send()
            face_copy(2 * a, 2 * a + 1, device(at + 1)).wait_recv()

        @pl.when(at > 0)
        def _():
            face_copy(2 * a, 2 * a + 1, device(at - 1)).wait_send()
            face_copy(2 * a + 1, 2 * a, device(at - 1)).wait_recv()

    pltpu.make_async_copy(src_s, src_s, src_sem.at[0]).wait()

    def split_near(p, to):
        for h in range(2):
            hi, lo = split(m2l_v[p * 2 + h])
            near_w[to, 0:coef, h * 128 : h * 128 + coef] = hi
            near_w[to, 128 : 128 + coef, h * 128 : h * 128 + coef] = lo

    arrive(m2l_v, 4)
    split_near(0, 0)

    def near(p, offs):
        @pl.when(p == UP_STEP)
        def _():
            lax.fori_loop(gz + 1, ngz, get_box, 0)
            lax.fori_loop(gz + 1, ngz, send_box, 0)

        pl.when(p == LINE_STEP)(line_done)

        def picked(h, n):
            v = src_s.at[lax.div(p, 4) * (ncell // 128) + n // 128, lax.rem(p, 4) * 2 + h, pl.ds(n % 128, 8)]
            return pick8(pool, lambda s: v[offs[s]], sub)

        now = lax.rem(p, 2)
        his, los = [], []
        for n in range(0, ncell, 16):
            rows = [jnp.concatenate([picked(h, n), picked(h, n + 8)], axis=0) for h in range(2)]
            hi, lo = split(jnp.concatenate(rows, axis=1))
            his.append(hi)
            los.append(lo)
        w = near_w[now]
        both = nt(jnp.concatenate(his, axis=0), w)
        low = nt(jnp.concatenate(los, axis=0), w[0:128])
        acc[...] += both[:, 0:128] + both[:, 128:256] + low
        split_near(jnp.minimum(p + 1, ops // 2 - 1), 1 - now)
        return offs

    lax.fori_loop(0, ops // 2, near, offs)

    all_of(plane, nplane, plane_send, plane_recv).wait()
    all_of(line, ngz, line_send, line_recv).wait_send()
    for i in range(nplane):
        boxes[i : i + 1, :] = plane[i]
    known_sibs = [sibs[s : s + 1, :] for s in range(5)]
    known_sibs.append(boxes[pl.ds(sibling(place, 0), 1), :])
    sixth = pair(sibling(place, 1))
    boxes[0:4, :] = quads(16)
    known_sibs.append(None)
    known_sibs.append(boxes[pl.ds(sibling(place, 2), 1), :])
    last = merged([sixth, pair(sibling(place, 3))])
    known_sibs[6] = last[0:1, :]
    known_sibs.append(last[1:2, :])
    every = jnp.concatenate(known_sibs, axis=1)
    g = dot3(every, far_w[0, :, 0 : levels * 128], far_w[1, :, 0 : levels * 128])
    spread = dot3(g, down_w[0], down_w[1])
    classes = jnp.concatenate([spread[0:1, o * 128 : (o + 1) * 128] for o in range(8)], axis=0)
    spread = jnp.concatenate([classes] * 16, axis=0).T
    for b in range(ncell // 128):
        block = acc[b * 128 : (b + 1) * 128, :].T + spread
        out[:, b * 128 : (b + 1) * 128] = block[0:coef, :]


def shards(mesh, multipoles, sources, halo_cells, m2l_ops, cell_up, cell_down, side_ops):
    coef, ncell = multipoles.shape
    ops = sources.shape[0]
    nhalo = halo_cells.shape[1]
    ngx, ngy, ngz = (mesh.shape[a] for a in AXES)
    nplane = ngx * ngy
    hbm = pl.BlockSpec(memory_space=pltpu.HBM)
    vmem, dma = pltpu.VMEM, pltpu.SemaphoreType.DMA
    m2l = jnp.transpose(m2l_ops, (1, 0, 2))
    up = jnp.transpose(cell_up, (1, 0, 2))
    down = jnp.transpose(cell_down, (1, 0, 2))
    side = jnp.transpose(side_ops, (0, 2, 1, 3))
    return pl.pallas_call(
        functools.partial(kernel, (coef, ncell, ops, nhalo, ngx, ngy, ngz)),
        out_shape=jax.ShapeDtypeStruct((coef, ncell), F32),
        in_specs=[hbm] * 7,
        out_specs=pl.BlockSpec(memory_space=vmem),
        scratch_shapes=[
            vmem((coef, ncell), F32),
            vmem((ncell, 128), F32),
            vmem((ncell + 6 * nhalo, 128), F32),
            vmem((6, nhalo, 128), F32),
            pltpu.SMEM((ops // 8 * (ncell // 128), 8, 128), jnp.int32),
            pltpu.SMEM((6, nhalo), jnp.int32),
            vmem((ops, coef, coef), F32),
            vmem((8, coef, coef), F32),
            vmem((8, coef, coef), F32),
            vmem((3, coef, 2, coef), F32),
            vmem((2, 256, 256), BF16),
            vmem((2, 128, 1024), BF16),
            vmem((2, 1024, 128), BF16),
            vmem((3, 2, 128, 128), F32),
            vmem((2, 128, 256), BF16),
            vmem((2, 128, 512), BF16),
            vmem((2, 128, 128 * 16), BF16),
            vmem((ncell, 128), F32),
            vmem((2, 1, 128), F32),
            vmem((ngz, 1, 128), F32),
            vmem((nplane, 1, 128), F32),
            vmem((ngz, 128), F32),
            vmem((16, 128), F32),
            dma((6,)),
            dma((1,)),
            dma((6,)),
            dma((6,)),
            dma((1,)),
            dma((ngz,)),
            dma((1,)),
            dma((1,)),
        ],
        compiler_params=pltpu.CompilerParams(
            collective_id=0, has_side_effects=True, vmem_limit_bytes=63 * 2**20
        ),
        cost_estimate=pl.CostEstimate(flops=3 * 10**9, bytes_accessed=4 * 10**6, transcendentals=0),
    )(multipoles, sources, halo_cells, m2l, up, down, side)


def solution(mesh):
    split_cells = P(None, AXES)
    split_rows = P(AXES, None)
    return jax.shard_map(
        functools.partial(shards, mesh),
        mesh=mesh,
        in_specs=(split_cells, split_rows, split_rows, P(), P(), P(), P()),
        out_specs=split_cells,
        check_vma=False,
    )
```

```python
import functools

import jax
import jax.numpy as jnp
from jax import lax
from jax.experimental import pallas as pl
from jax.experimental.pallas import tpu as pltpu
from jax.sharding import PartitionSpec as P

F32, BF16 = jnp.float32, jnp.bfloat16
MESH = pl.DeviceIdType.MESH
NT = (((1,), (1,)), ((), ()))
AXES = ("gx", "gy", "gz")
UP_PAIR = 9
LINE_PAIR = 12


def split(x):
    hi = x.astype(BF16)
    return hi, (x - hi.astype(F32)).astype(BF16)


def nt(a, b):
    return lax.dot_general(a, b, NT, preferred_element_type=F32)


def dot3(x, wide, narrow):
    hi, lo = split(x)
    return nt(hi, wide) + (nt(lo, wide) + nt(hi, narrow))


def nn3(a, b):
    ah, al = split(a)
    bh, bl = split(b)
    dot = functools.partial(jnp.dot, preferred_element_type=F32)
    return dot(ah, bh) + (dot(al, bh) + dot(ah, bl))


def pick8(table, index_of, sub):
    block = None
    for s in range(8):
        row = jnp.broadcast_to(table[pl.ds(index_of(s), 1), :], (8, 128))
        block = row if block is None else jnp.where(sub == s, row, block)
    return block


def kernel(
    sizes, mult, sources, halo, m2l, up, down, side, out,
    cells, own, pool, faces, src_s, halo_s, m2l_v, up_v, down_v, side_v,
    near_w, up_w, down_w, side_w, merge_w, merge4_w, far_w, acc,
    mine, line, plane, boxes, sibs,
    in_sem, src_sem, face_send, face_recv, line_send, line_recv, plane_send, plane_recv,
):
    coef, ncell, ops, nhalo, ngx, ngy, ngz = sizes
    nplane = ngx * ngy
    gx, gy, gz = (lax.axis_index(a) for a in AXES)
    place = gx * ngy + gy
    me = place * ngz + gz
    zero = lax.shift_right_logical(me, 24)
    offs = tuple(zero + j for j in range(8))
    sub = lax.broadcasted_iota(jnp.int32, (8, 128), 0)

    loads = [
        pltpu.make_async_copy(mult, cells, in_sem.at[0]),
        pltpu.make_async_copy(halo, halo_s, in_sem.at[1]),
        pltpu.make_async_copy(side, side_v, in_sem.at[3]),
    ]
    loads[0].start()
    loads[1].start()

    def slices(table, to, sem):
        def one(k, c):
            pltpu.make_async_copy(table.at[:, k, :], to.at[k], in_sem.at[sem]).start()
            return c

        lax.fori_loop(0, to.shape[0], one, 0)

    def arrive(to, sem):
        pltpu.make_async_copy(to, to, in_sem.at[sem]).wait()

    def rows_of(k, place):
        return pltpu.make_async_copy(sources.at[k], src_s[place], src_sem.at[place])

    barrier = pltpu.get_barrier_semaphore()

    def in_plane(j):
        other = lax.rem(place + j, nplane)
        return {"gx": lax.div(other, ngy), "gy": lax.rem(other, ngy)}

    def greet(device):
        pl.semaphore_signal(barrier, inc=1, device_id=device, device_id_type=MESH)

    def greet_plane(j, c):
        greet(in_plane(j))
        return c

    def greet_up(i, c):
        greet({"gz": i})
        return c

    pl.when(gz > 0)(lambda: greet({"gz": gz - 1}))
    lax.fori_loop(gz + 1, ngz, greet_up, 0)
    lax.fori_loop(1, nplane, greet_plane, 0)
    greeted = nplane - 1 + gz + (gz < ngz - 1).astype(jnp.int32)

    loads[0].wait()
    for b in range(ncell // 128):
        block = jnp.concatenate(
            [cells[:, b * 128 : (b + 1) * 128], jnp.zeros((128 - coef, 128), F32)], axis=0
        ).T
        own[b * 128 : (b + 1) * 128, :] = block
        pool[b * 128 : (b + 1) * 128, :] = block

    slices(up, up_v, 2)
    loads[2].start()
    slices(down, down_v, 5)
    slices(m2l, m2l_v, 4)
    loads[1].wait()
    neighbours = (
        (gx, ngx, lambda i: {"gx": i}),
        (gy, ngy, lambda i: {"gy": i}),
        (gz, ngz, lambda i: {"gz": i}),
    )

    def slot(i):
        return pool.at[pl.ds(ncell + i * nhalo, nhalo)]

    def face_copy(face, land, device):
        return pltpu.make_async_remote_copy(
            src_ref=faces.at[face],
            dst_ref=slot(land),
            send_sem=face_send.at[face],
            recv_sem=face_recv.at[land],
            device_id=device,
            device_id_type=MESH,
        )

    def gather_face(face):
        def part(i, c):
            for r in range(16):
                v = halo_s.at[face, pl.ds(i * 128 + r * 8, 8)]
                faces[face, pl.ds(pl.multiple_of(i * 128 + r * 8, 8), 8), :] = pick8(
                    own, lambda s: v[offs[s]], sub
                )
            return c

        lax.fori_loop(0, nhalo // 128, part, 0)

    for a, (at, count, device) in enumerate(neighbours):
        gather_face(2 * a)
        gather_face(2 * a + 1)
        if a == 0:
            pl.semaphore_wait(barrier, greeted)

        @pl.when(at < count - 1)
        def _():
            face_copy(2 * a + 1, 2 * a, device(at + 1)).start()

        @pl.when(at > 0)
        def _():
            face_copy(2 * a, 2 * a + 1, device(at - 1)).start()

    for k in range(4):
        rows_of(k, k).start()

    up_w[...] = jnp.zeros_like(up_w)
    arrive(up_v, 2)
    for o in range(8):
        hi, lo = split(up_v[o])
        up_w[0, 0:coef, o * 128 : o * 128 + coef] = hi
        up_w[1, 0:coef, o * 128 : o * 128 + coef] = lo

    def add_class(i, total):
        for r in range(16):
            total = total + own[pl.ds(pl.multiple_of(i * 128 + r * 8, 8), 8), :]
        return total

    classes = lax.fori_loop(0, ncell // 128, add_class, jnp.zeros((8, 128), F32))
    flat = jnp.concatenate([classes[o : o + 1, :] for o in range(8)], axis=1)
    box = dot3(jnp.broadcast_to(flat, (8, 1024)), up_w[0], up_w[1])
    mine[0] = box[0:1, :]

    def line_copy(sender, device):
        return pltpu.make_async_remote_copy(
            src_ref=mine.at[0],
            dst_ref=line.at[sender],
            send_sem=line_send.at[0],
            recv_sem=line_recv.at[sender],
            device_id={"gz": device},
            device_id_type=MESH,
        )

    def send_box(to, c):
        line_copy(gz, to).start()
        return c

    def get_box(sender, c):
        line_copy(sender, sender).wait_recv()
        return c

    lax.fori_loop(0, gz, send_box, 0)
    line[gz] = box[0:1, :]

    for a, (at, count, _) in enumerate(neighbours):
        @pl.when(at == 0)
        def _():
            slot(2 * a)[...] = jnp.zeros((nhalo, 128), F32)

        @pl.when(at == count - 1)
        def _():
            slot(2 * a + 1)[...] = jnp.zeros((nhalo, 128), F32)

    for w in (down_w, side_w, near_w):
        w[...] = jnp.zeros_like(w)

    loads[2].wait()
    for a in range(3):
        for b in range(2):
            side_w[a, b, 0:coef, 0:coef] = side_v[a, :, b, :]
    merge = jnp.concatenate([side_w[0, 0], side_w[0, 1]], axis=1)
    merge_w[0], merge_w[1] = split(merge)
    four = nn3(jnp.concatenate([side_w[0, 0], side_w[0, 1]], axis=0), merge)
    merge4_w[0], merge4_w[1] = split(jnp.concatenate([four[0:128], four[128:256]], axis=1))
    levels = (ngz * nplane).bit_length() - 1
    turn = [lax.rem(lax.shift_right_logical(me, s), 2) for s in range(levels)]
    step = [side_w[2, turn[s]] for s in range(levels)]
    two = [nn3(step[s], step[s + 1]) for s in range(0, levels - 1, 2)]
    third = nn3(two[0], jnp.concatenate([step[2], two[1]], axis=1))
    rest = nn3(two[2], jnp.concatenate([step[6], two[3]], axis=1))
    upper = nn3(third[:, 128:256], jnp.concatenate([step[4], two[2], rest], axis=1))
    way = [None, step[0], two[0], third[:, 0:128], third[:, 128:256]]
    way += [upper[:, i * 128 : (i + 1) * 128] for i in range(4)]
    for s in range(levels):
        cross = side_w[1, turn[s]]
        far_w[0, :, s * 128 : (s + 1) * 128], far_w[1, :, s * 128 : (s + 1) * 128] = split(
            nn3(way[s], cross) if s else cross
        )
    arrive(down_v, 5)
    for o in range(8):
        hi, lo = split(down_v[o])
        down_w[0, o * 128 : o * 128 + coef, 0:coef] = hi
        down_w[1, o * 128 : o * 128 + coef, 0:coef] = lo
    acc[...] = jnp.zeros_like(acc)
    sibs[...] = jnp.zeros_like(sibs)

    def plane_copy(j):
        return pltpu.make_async_remote_copy(
            src_ref=mine.at[1],
            dst_ref=plane.at[place],
            send_sem=plane_send.at[0],
            recv_sem=plane_recv.at[0],
            device_id=in_plane(j),
            device_id_type=MESH,
        )

    def send_top(j, c):
        plane_copy(j).start()
        return c

    def all_of(buffer, count, send, recv):
        every = buffer.at[pl.ds(0, count - 1)]
        return pltpu.make_async_remote_copy(
            src_ref=every,
            dst_ref=every,
            send_sem=send.at[0],
            recv_sem=recv.at[0],
            device_id=in_plane(1),
            device_id_type=MESH,
        )

    def quads(count):
        rows = [boxes[pl.ds(i, count // 4, 4), :] for i in range(4)]
        return dot3(jnp.concatenate(rows, axis=1), merge4_w[0], merge4_w[1])

    def pair(index):
        return jnp.concatenate([boxes[pl.ds(2 * index, 1), :], boxes[pl.ds(2 * index + 1, 1), :]], axis=1)

    def merged(rows):
        return dot3(jnp.concatenate(rows, axis=0), merge_w[0], merge_w[1])

    def sibling(index, s):
        mask = lax.shift_right_logical(index, s)
        return mask + 1 - 2 * lax.rem(mask, 2)

    def line_done():
        lax.fori_loop(0, gz, get_box, 0)
        for i in range(ngz):
            boxes[i : i + 1, :] = line[i]
        sibs[0:1, :] = boxes[pl.ds(sibling(gz, 0), 1), :]
        first = pair(sibling(gz, 1))
        boxes[0:8, :] = quads(32)
        sibs[2:3, :] = boxes[pl.ds(sibling(gz, 2), 1), :]
        third = pair(sibling(gz, 3))
        boxes[0:2, :] = quads(8)
        sibs[4:5, :] = boxes[pl.ds(sibling(gz, 4), 1), :]
        top = merged([first, third, pair(0)])
        sibs[1:2, :] = top[0:1, :]
        sibs[3:4, :] = top[1:2, :]
        mine[1] = top[2:3, :]
        plane[place] = top[2:3, :]
        lax.fori_loop(1, nplane, send_top, 0)

    for a, (at, count, device) in enumerate(neighbours):
        @pl.when(at < count - 1)
        def _():
            face_copy(2 * a + 1, 2 * a, device(at + 1)).wait_send()
            face_copy(2 * a, 2 * a + 1, device(at + 1)).wait_recv()

        @pl.when(at > 0)
        def _():
            face_copy(2 * a, 2 * a + 1, device(at - 1)).wait_send()
            face_copy(2 * a + 1, 2 * a, device(at - 1)).wait_recv()


    def split_near(p, to):
        for h in range(2):
            hi, lo = split(m2l_v[p * 2 + h])
            near_w[to, 0:coef, h * 128 : h * 128 + coef] = hi
            near_w[to, 128 : 128 + coef, h * 128 : h * 128 + coef] = lo

    arrive(m2l_v, 4)
    split_near(0, 0)

    def near_pair(p, half):
        def picked(h, n):
            return pick8(pool, lambda s: src_s[2 * half + h][n + s], sub)

        for h in range(2):
            rows_of(2 * p + h, 2 * half + h).wait()
        his, los = [], []
        for n in range(0, ncell, 16):
            rows = [jnp.concatenate([picked(h, n), picked(h, n + 8)], axis=0) for h in range(2)]
            hi, lo = split(jnp.concatenate(rows, axis=1))
            his.append(hi)
            los.append(lo)

        @pl.when(p + 2 < ops // 2)
        def _():
            for h in range(2):
                rows_of(2 * p + 4 + h, 2 * half + h).start()

        w = near_w[half]
        both = nt(jnp.concatenate(his, axis=0), w)
        low = nt(jnp.concatenate(los, axis=0), w[0:128])
        acc[...] += both[:, 0:128] + both[:, 128:256] + low
        split_near(jnp.minimum(p + 1, ops // 2 - 1), 1 - half)

    def hear_above():
        lax.fori_loop(gz + 1, ngz, get_box, 0)
        lax.fori_loop(gz + 1, ngz, send_box, 0)

    def near(i, c):
        for half in range(2):
            for pair_number, hook in ((UP_PAIR, hear_above), (LINE_PAIR, line_done)):
                if pair_number % 2 == half:
                    pl.when(i == pair_number // 2)(hook)
            near_pair(2 * i + half, half)
        return c

    lax.fori_loop(0, ops // 4, near, 0)

    all_of(plane, nplane, plane_send, plane_recv).wait()
    all_of(line, ngz, line_send, line_recv).wait_send()
    for i in range(nplane):
        boxes[i : i + 1, :] = plane[i]
    known_sibs = [sibs[s : s + 1, :] for s in range(5)]
    known_sibs.append(boxes[pl.ds(sibling(place, 0), 1), :])
    sixth = pair(sibling(place, 1))
    boxes[0:4, :] = quads(16)
    known_sibs.append(None)
    known_sibs.append(boxes[pl.ds(sibling(place, 2), 1), :])
    last = merged([sixth, pair(sibling(place, 3))])
    known_sibs[6] = last[0:1, :]
    known_sibs.append(last[1:2, :])
    every = jnp.concatenate(known_sibs, axis=1)
    g = dot3(every, far_w[0, :, 0 : levels * 128], far_w[1, :, 0 : levels * 128])
    spread = dot3(g, down_w[0], down_w[1])
    classes = jnp.concatenate([spread[0:1, o * 128 : (o + 1) * 128] for o in range(8)], axis=0)
    spread = jnp.concatenate([classes] * 16, axis=0).T
    for b in range(ncell // 128):
        block = acc[b * 128 : (b + 1) * 128, :].T + spread
        out[:, b * 128 : (b + 1) * 128] = block[0:coef, :]


def shards(mesh, multipoles, sources, halo_cells, m2l_ops, cell_up, cell_down, side_ops):
    coef, ncell = multipoles.shape
    ops = sources.shape[0]
    nhalo = halo_cells.shape[1]
    ngx, ngy, ngz = (mesh.shape[a] for a in AXES)
    nplane = ngx * ngy
    hbm = pl.BlockSpec(memory_space=pltpu.HBM)
    vmem, dma = pltpu.VMEM, pltpu.SemaphoreType.DMA
    m2l = jnp.transpose(m2l_ops, (1, 0, 2))
    up = jnp.transpose(cell_up, (1, 0, 2))
    down = jnp.transpose(cell_down, (1, 0, 2))
    side = jnp.transpose(side_ops, (0, 2, 1, 3))
    return pl.pallas_call(
        functools.partial(kernel, (coef, ncell, ops, nhalo, ngx, ngy, ngz)),
        out_shape=jax.ShapeDtypeStruct((coef, ncell), F32),
        in_specs=[hbm] * 7,
        out_specs=pl.BlockSpec(memory_space=vmem),
        scratch_shapes=[
            vmem((coef, ncell), F32),
            vmem((ncell, 128), F32),
            vmem((ncell + 6 * nhalo, 128), F32),
            vmem((6, nhalo, 128), F32),
            [pltpu.SMEM((ncell,), jnp.int32)] * 4,
            pltpu.SMEM((6, nhalo), jnp.int32),
            vmem((ops, coef, coef), F32),
            vmem((8, coef, coef), F32),
            vmem((8, coef, coef), F32),
            vmem((3, coef, 2, coef), F32),
            vmem((2, 256, 256), BF16),
            vmem((2, 128, 1024), BF16),
            vmem((2, 1024, 128), BF16),
            vmem((3, 2, 128, 128), F32),
            vmem((2, 128, 256), BF16),
            vmem((2, 128, 512), BF16),
            vmem((2, 128, 128 * 16), BF16),
            vmem((ncell, 128), F32),
            vmem((2, 1, 128), F32),
            vmem((ngz, 1, 128), F32),
            vmem((nplane, 1, 128), F32),
            vmem((ngz, 128), F32),
            vmem((16, 128), F32),
            dma((6,)),
            dma((4,)),
            dma((6,)),
            dma((6,)),
            dma((1,)),
            dma((ngz,)),
            dma((1,)),
            dma((1,)),
        ],
        compiler_params=pltpu.CompilerParams(
            collective_id=0, has_side_effects=True, vmem_limit_bytes=63 * 2**20
        ),
        cost_estimate=pl.CostEstimate(flops=3 * 10**9, bytes_accessed=4 * 10**6, transcendentals=0),
    )(multipoles, sources, halo_cells, m2l, up, down, side)


def solution(mesh):
    split_cells = P(None, AXES)
    split_rows = P(AXES, None)
    return jax.shard_map(
        functools.partial(shards, mesh),
        mesh=mesh,
        in_specs=(split_cells, split_rows, split_rows, P(), P(), P(), P()),
        out_specs=split_cells,
        check_vma=False,
    )
```

```python
import functools

import jax
import jax.numpy as jnp
from jax import lax
from jax.experimental import pallas as pl
from jax.experimental.pallas import tpu as pltpu
from jax.sharding import PartitionSpec as P

F32, BF16 = jnp.float32, jnp.bfloat16
MESH = pl.DeviceIdType.MESH
NT = (((1,), (1,)), ((), ()))
AXES = ("gx", "gy", "gz")
UP_PAIR = 10
LINE_PAIR = 13


def split(x):
    hi = x.astype(BF16)
    return hi, (x - hi.astype(F32)).astype(BF16)


def nt(a, b):
    return lax.dot_general(a, b, NT, preferred_element_type=F32)


def dot3(x, wide, narrow):
    hi, lo = split(x)
    return nt(hi, wide) + (nt(lo, wide) + nt(hi, narrow))


def nn3(a, b):
    ah, al = split(a)
    bh, bl = split(b)
    dot = functools.partial(jnp.dot, preferred_element_type=F32)
    return dot(ah, bh) + (dot(al, bh) + dot(ah, bl))


def pick8(table, index_of, sub):
    block = None
    for s in range(8):
        row = jnp.broadcast_to(table[pl.ds(index_of(s), 1), :], (8, 128))
        block = row if block is None else jnp.where(sub == s, row, block)
    return block


def kernel(
    sizes, mult, sources, halo, m2l, up, down, side, out,
    cells, own, pool, faces, src_s, halo_s, m2l_v, up_v, down_v, side_v,
    near_w, up_w, down_w, side_w, merge_w, merge4_w, far_w, acc,
    mine, line, plane, boxes, sibs,
    in_sem, src_sem, face_send, face_recv, line_send, line_recv, plane_send, plane_recv,
):
    coef, ncell, ops, nhalo, ngx, ngy, ngz = sizes
    nplane = ngx * ngy
    gx, gy, gz = (lax.axis_index(a) for a in AXES)
    place = gx * ngy + gy
    me = place * ngz + gz
    zero = lax.shift_right_logical(me, 24)
    offs = tuple(zero + j for j in range(8))
    sub = lax.broadcasted_iota(jnp.int32, (8, 128), 0)

    loads = [
        pltpu.make_async_copy(mult, cells, in_sem.at[0]),
        pltpu.make_async_copy(halo, halo_s, in_sem.at[1]),
        pltpu.make_async_copy(side, side_v, in_sem.at[3]),
    ]
    loads[0].start()
    loads[1].start()

    def slices(table, to, sem):
        def one(k, c):
            pltpu.make_async_copy(table.at[:, k, :], to.at[k], in_sem.at[sem]).start()
            return c

        lax.fori_loop(0, to.shape[0], one, 0)

    def arrive(to, sem):
        pltpu.make_async_copy(to, to, in_sem.at[sem]).wait()

    def rows_of(k, place):
        return pltpu.make_async_copy(sources.at[k], src_s[place], src_sem.at[place])

    barrier = pltpu.get_barrier_semaphore()

    def in_plane(j):
        other = lax.rem(place + j, nplane)
        return {"gx": lax.div(other, ngy), "gy": lax.rem(other, ngy)}

    def greet(device):
        pl.semaphore_signal(barrier, inc=1, device_id=device, device_id_type=MESH)

    def greet_plane(j, c):
        greet(in_plane(j))
        return c

    def greet_up(i, c):
        greet({"gz": i})
        return c

    pl.when(gz > 0)(lambda: greet({"gz": gz - 1}))
    lax.fori_loop(gz + 1, ngz, greet_up, 0)
    lax.fori_loop(1, nplane, greet_plane, 0)
    greeted = nplane - 1 + gz + (gz < ngz - 1).astype(jnp.int32)

    loads[0].wait()
    for b in range(ncell // 128):
        block = jnp.concatenate(
            [cells[:, b * 128 : (b + 1) * 128], jnp.zeros((128 - coef, 128), F32)], axis=0
        ).T
        own[b * 128 : (b + 1) * 128, :] = block
        pool[b * 128 : (b + 1) * 128, :] = block

    slices(up, up_v, 2)
    loads[2].start()
    slices(down, down_v, 5)
    slices(m2l, m2l_v, 4)
    loads[1].wait()
    neighbours = (
        (gx, ngx, lambda i: {"gx": i}),
        (gy, ngy, lambda i: {"gy": i}),
        (gz, ngz, lambda i: {"gz": i}),
    )

    def slot(i):
        return pool.at[pl.ds(ncell + i * nhalo, nhalo)]

    def face_copy(face, land, device):
        return pltpu.make_async_remote_copy(
            src_ref=faces.at[face],
            dst_ref=slot(land),
            send_sem=face_send.at[face],
            recv_sem=face_recv.at[land],
            device_id=device,
            device_id_type=MESH,
        )

    def gather_face(face):
        def part(i, c):
            for r in range(16):
                v = halo_s.at[face, pl.ds(i * 128 + r * 8, 8)]
                faces[face, pl.ds(pl.multiple_of(i * 128 + r * 8, 8), 8), :] = pick8(
                    own, lambda s: v[offs[s]], sub
                )
            return c

        lax.fori_loop(0, nhalo // 128, part, 0)

    for a, (at, count, device) in enumerate(neighbours):
        gather_face(2 * a)
        gather_face(2 * a + 1)
        if a == 0:
            pl.semaphore_wait(barrier, greeted)

        @pl.when(at < count - 1)
        def _():
            face_copy(2 * a + 1, 2 * a, device(at + 1)).start()

        @pl.when(at > 0)
        def _():
            face_copy(2 * a, 2 * a + 1, device(at - 1)).start()

    for k in range(4):
        rows_of(k, k).start()

    up_w[...] = jnp.zeros_like(up_w)
    arrive(up_v, 2)
    for o in range(8):
        hi, lo = split(up_v[o])
        up_w[0, 0:coef, o * 128 : o * 128 + coef] = hi
        up_w[1, 0:coef, o * 128 : o * 128 + coef] = lo

    def add_class(i, total):
        for r in range(16):
            total = total + own[pl.ds(pl.multiple_of(i * 128 + r * 8, 8), 8), :]
        return total

    classes = lax.fori_loop(0, ncell // 128, add_class, jnp.zeros((8, 128), F32))
    flat = jnp.concatenate([classes[o : o + 1, :] for o in range(8)], axis=1)
    box = dot3(jnp.broadcast_to(flat, (8, 1024)), up_w[0], up_w[1])
    mine[0] = box[0:1, :]

    def line_copy(sender, device):
        return pltpu.make_async_remote_copy(
            src_ref=mine.at[0],
            dst_ref=line.at[sender],
            send_sem=line_send.at[0],
            recv_sem=line_recv.at[sender],
            device_id={"gz": device},
            device_id_type=MESH,
        )

    def send_box(to, c):
        line_copy(gz, to).start()
        return c

    def get_box(sender, c):
        line_copy(sender, sender).wait_recv()
        return c

    line[gz] = box[0:1, :]

    for a, (at, count, _) in enumerate(neighbours):
        @pl.when(at == 0)
        def _():
            slot(2 * a)[...] = jnp.zeros((nhalo, 128), F32)

        @pl.when(at == count - 1)
        def _():
            slot(2 * a + 1)[...] = jnp.zeros((nhalo, 128), F32)

    for w in (down_w, side_w, near_w):
        w[...] = jnp.zeros_like(w)

    loads[2].wait()
    for a in range(3):
        for b in range(2):
            side_w[a, b, 0:coef, 0:coef] = side_v[a, :, b, :]
    merge = jnp.concatenate([side_w[0, 0], side_w[0, 1]], axis=1)
    merge_w[0], merge_w[1] = split(merge)
    four = nn3(jnp.concatenate([side_w[0, 0], side_w[0, 1]], axis=0), merge)
    merge4_w[0], merge4_w[1] = split(jnp.concatenate([four[0:128], four[128:256]], axis=1))
    levels = (ngz * nplane).bit_length() - 1
    turn = [lax.rem(lax.shift_right_logical(me, s), 2) for s in range(levels)]
    step = [side_w[2, turn[s]] for s in range(levels)]
    two = [nn3(step[s], step[s + 1]) for s in range(0, levels - 1, 2)]
    third = nn3(two[0], jnp.concatenate([step[2], two[1]], axis=1))
    rest = nn3(two[2], jnp.concatenate([step[6], two[3]], axis=1))
    upper = nn3(third[:, 128:256], jnp.concatenate([step[4], two[2], rest], axis=1))
    way = [None, step[0], two[0], third[:, 0:128], third[:, 128:256]]
    way += [upper[:, i * 128 : (i + 1) * 128] for i in range(4)]
    for s in range(levels):
        cross = side_w[1, turn[s]]
        far_w[0, :, s * 128 : (s + 1) * 128], far_w[1, :, s * 128 : (s + 1) * 128] = split(
            nn3(way[s], cross) if s else cross
        )
    arrive(down_v, 5)
    for o in range(8):
        hi, lo = split(down_v[o])
        down_w[0, o * 128 : o * 128 + coef, 0:coef] = hi
        down_w[1, o * 128 : o * 128 + coef, 0:coef] = lo
    acc[...] = jnp.zeros_like(acc)
    sibs[...] = jnp.zeros_like(sibs)

    def plane_copy(j):
        return pltpu.make_async_remote_copy(
            src_ref=mine.at[1],
            dst_ref=plane.at[place],
            send_sem=plane_send.at[0],
            recv_sem=plane_recv.at[0],
            device_id=in_plane(j),
            device_id_type=MESH,
        )

    def send_top(j, c):
        plane_copy(j).start()
        return c

    def all_of(buffer, count, send, recv):
        every = buffer.at[pl.ds(0, count - 1)]
        return pltpu.make_async_remote_copy(
            src_ref=every,
            dst_ref=every,
            send_sem=send.at[0],
            recv_sem=recv.at[0],
            device_id=in_plane(1),
            device_id_type=MESH,
        )

    def quads(count):
        rows = [boxes[pl.ds(i, count // 4, 4), :] for i in range(4)]
        return dot3(jnp.concatenate(rows, axis=1), merge4_w[0], merge4_w[1])

    def pair(index):
        return jnp.concatenate([boxes[pl.ds(2 * index, 1), :], boxes[pl.ds(2 * index + 1, 1), :]], axis=1)

    def merged(rows):
        return dot3(jnp.concatenate(rows, axis=0), merge_w[0], merge_w[1])

    def sibling(index, s):
        mask = lax.shift_right_logical(index, s)
        return mask + 1 - 2 * lax.rem(mask, 2)

    def line_done():
        lax.fori_loop(0, gz, get_box, 0)
        for i in range(ngz):
            boxes[i : i + 1, :] = line[i]
        sibs[0:1, :] = boxes[pl.ds(sibling(gz, 0), 1), :]
        first = pair(sibling(gz, 1))
        boxes[0:8, :] = quads(32)
        sibs[2:3, :] = boxes[pl.ds(sibling(gz, 2), 1), :]
        third = pair(sibling(gz, 3))
        boxes[0:2, :] = quads(8)
        sibs[4:5, :] = boxes[pl.ds(sibling(gz, 4), 1), :]
        top = merged([first, third, pair(0)])
        sibs[1:2, :] = top[0:1, :]
        sibs[3:4, :] = top[1:2, :]
        mine[1] = top[2:3, :]
        plane[place] = top[2:3, :]
        lax.fori_loop(1, nplane, send_top, 0)

    for a, (at, count, device) in enumerate(neighbours):
        @pl.when(at < count - 1)
        def _():
            face_copy(2 * a + 1, 2 * a, device(at + 1)).wait_send()
            face_copy(2 * a, 2 * a + 1, device(at + 1)).wait_recv()

        @pl.when(at > 0)
        def _():
            face_copy(2 * a, 2 * a + 1, device(at - 1)).wait_send()
            face_copy(2 * a + 1, 2 * a, device(at - 1)).wait_recv()


    def split_near(p, to):
        for h in range(2):
            hi, lo = split(m2l_v[p * 2 + h])
            near_w[to, 0:coef, h * 128 : h * 128 + coef] = hi
            near_w[to, 128 : 128 + coef, h * 128 : h * 128 + coef] = lo

    arrive(m2l_v, 4)
    split_near(0, 0)

    lax.fori_loop(0, gz, send_box, 0)

    def near_pair(p, half):
        def picked(h, n):
            return pick8(pool, lambda s: src_s[2 * half + h][n + s], sub)

        for h in range(2):
            rows_of(2 * p + h, 2 * half + h).wait()
        his, los = [], []
        for n in range(0, ncell, 16):
            rows = [jnp.concatenate([picked(h, n), picked(h, n + 8)], axis=0) for h in range(2)]
            hi, lo = split(jnp.concatenate(rows, axis=1))
            his.append(hi)
            los.append(lo)

        @pl.when(p + 2 < ops // 2)
        def _():
            for h in range(2):
                rows_of(2 * p + 4 + h, 2 * half + h).start()

        w = near_w[half]
        both = nt(jnp.concatenate(his, axis=0), w)
        low = nt(jnp.concatenate(los, axis=0), w[0:128])
        acc[...] += both[:, 0:128] + both[:, 128:256] + low
        split_near(jnp.minimum(p + 1, ops // 2 - 1), 1 - half)

    def hear_above():
        lax.fori_loop(gz + 1, ngz, get_box, 0)
        lax.fori_loop(gz + 1, ngz, send_box, 0)

    def near(i, c):
        for half in range(2):
            for pair_number, hook in ((UP_PAIR, hear_above), (LINE_PAIR, line_done)):
                if pair_number % 2 == half:
                    pl.when(i == pair_number // 2)(hook)
            near_pair(2 * i + half, half)
        return c

    lax.fori_loop(0, ops // 4, near, 0)

    all_of(plane, nplane, plane_send, plane_recv).wait()
    all_of(line, ngz, line_send, line_recv).wait_send()
    for i in range(nplane):
        boxes[i : i + 1, :] = plane[i]
    known_sibs = [sibs[s : s + 1, :] for s in range(5)]
    known_sibs.append(boxes[pl.ds(sibling(place, 0), 1), :])
    sixth = pair(sibling(place, 1))
    boxes[0:4, :] = quads(16)
    known_sibs.append(None)
    known_sibs.append(boxes[pl.ds(sibling(place, 2), 1), :])
    last = merged([sixth, pair(sibling(place, 3))])
    known_sibs[6] = last[0:1, :]
    known_sibs.append(last[1:2, :])
    every = jnp.concatenate(known_sibs, axis=1)
    g = dot3(every, far_w[0, :, 0 : levels * 128], far_w[1, :, 0 : levels * 128])
    spread = dot3(g, down_w[0], down_w[1])
    classes = jnp.concatenate([spread[0:1, o * 128 : (o + 1) * 128] for o in range(8)], axis=0)
    spread = jnp.concatenate([classes] * 16, axis=0).T
    for b in range(ncell // 128):
        block = acc[b * 128 : (b + 1) * 128, :].T + spread
        out[:, b * 128 : (b + 1) * 128] = block[0:coef, :]


def shards(mesh, multipoles, sources, halo_cells, m2l_ops, cell_up, cell_down, side_ops):
    coef, ncell = multipoles.shape
    ops = sources.shape[0]
    nhalo = halo_cells.shape[1]
    ngx, ngy, ngz = (mesh.shape[a] for a in AXES)
    nplane = ngx * ngy
    hbm = pl.BlockSpec(memory_space=pltpu.HBM)
    vmem, dma = pltpu.VMEM, pltpu.SemaphoreType.DMA
    m2l = jnp.transpose(m2l_ops, (1, 0, 2))
    up = jnp.transpose(cell_up, (1, 0, 2))
    down = jnp.transpose(cell_down, (1, 0, 2))
    side = jnp.transpose(side_ops, (0, 2, 1, 3))
    return pl.pallas_call(
        functools.partial(kernel, (coef, ncell, ops, nhalo, ngx, ngy, ngz)),
        out_shape=jax.ShapeDtypeStruct((coef, ncell), F32),
        in_specs=[hbm] * 7,
        out_specs=pl.BlockSpec(memory_space=vmem),
        scratch_shapes=[
            vmem((coef, ncell), F32),
            vmem((ncell, 128), F32),
            vmem((ncell + 6 * nhalo, 128), F32),
            vmem((6, nhalo, 128), F32),
            [pltpu.SMEM((ncell,), jnp.int32)] * 4,
            pltpu.SMEM((6, nhalo), jnp.int32),
            vmem((ops, coef, coef), F32),
            vmem((8, coef, coef), F32),
            vmem((8, coef, coef), F32),
            vmem((3, coef, 2, coef), F32),
            vmem((2, 256, 256), BF16),
            vmem((2, 128, 1024), BF16),
            vmem((2, 1024, 128), BF16),
            vmem((3, 2, 128, 128), F32),
            vmem((2, 128, 256), BF16),
            vmem((2, 128, 512), BF16),
            vmem((2, 128, 128 * 16), BF16),
            vmem((ncell, 128), F32),
            vmem((2, 1, 128), F32),
            vmem((ngz, 1, 128), F32),
            vmem((nplane, 1, 128), F32),
            vmem((ngz, 128), F32),
            vmem((16, 128), F32),
            dma((6,)),
            dma((4,)),
            dma((6,)),
            dma((6,)),
            dma((1,)),
            dma((ngz,)),
            dma((1,)),
            dma((1,)),
        ],
        compiler_params=pltpu.CompilerParams(
            collective_id=0, has_side_effects=True, vmem_limit_bytes=63 * 2**20
        ),
        cost_estimate=pl.CostEstimate(flops=3 * 10**9, bytes_accessed=4 * 10**6, transcendentals=0),
    )(multipoles, sources, halo_cells, m2l, up, down, side)


def solution(mesh):
    split_cells = P(None, AXES)
    split_rows = P(AXES, None)
    return jax.shard_map(
        functools.partial(shards, mesh),
        mesh=mesh,
        in_specs=(split_cells, split_rows, split_rows, P(), P(), P(), P()),
        out_specs=split_cells,
        check_vma=False,
    )
```

```python
import functools

import jax
import jax.numpy as jnp
from jax import lax
from jax.experimental import pallas as pl
from jax.experimental.pallas import tpu as pltpu
from jax.sharding import PartitionSpec as P

F32, BF16 = jnp.float32, jnp.bfloat16
MESH = pl.DeviceIdType.MESH
NT = (((1,), (1,)), ((), ()))
AXES = ("gx", "gy", "gz")
UP_PAIR = 10
LINE_PAIR = 13


def split(x):
    hi = x.astype(BF16)
    return hi, (x - hi.astype(F32)).astype(BF16)


def nt(a, b):
    return lax.dot_general(a, b, NT, preferred_element_type=F32)


def dot3(x, wide, narrow):
    hi, lo = split(x)
    return nt(hi, wide) + (nt(lo, wide) + nt(hi, narrow))


def nn3(a, b):
    ah, al = split(a)
    bh, bl = split(b)
    dot = functools.partial(jnp.dot, preferred_element_type=F32)
    return dot(ah, bh) + (dot(al, bh) + dot(ah, bl))


def pick8(table, index_of, sub):
    block = None
    for s in range(8):
        row = jnp.broadcast_to(table[pl.ds(index_of(s), 1), :], (8, 128))
        block = row if block is None else jnp.where(sub == s, row, block)
    return block


def kernel(
    sizes, mult, sources, halo, m2l, up, down, side, out,
    cells, own, pool, faces, src_s, halo_s, m2l_v, up_v, down_v, side_v,
    near_w, up_w, down_w, side_w, merge_w, merge4_w, far_w, acc,
    mine, line, plane, boxes, sibs,
    in_sem, src_sem, face_send, face_recv, line_send, line_recv, plane_send, plane_recv,
):
    coef, ncell, ops, nhalo, ngx, ngy, ngz = sizes
    nplane = ngx * ngy
    gx, gy, gz = (lax.axis_index(a) for a in AXES)
    place = gx * ngy + gy
    me = place * ngz + gz
    zero = lax.shift_right_logical(me, 24)
    offs = tuple(zero + j for j in range(8))
    sub = lax.broadcasted_iota(jnp.int32, (8, 128), 0)

    loads = [
        pltpu.make_async_copy(mult, cells, in_sem.at[0]),
        pltpu.make_async_copy(halo, halo_s, in_sem.at[1]),
        pltpu.make_async_copy(side, side_v, in_sem.at[3]),
    ]
    loads[0].start()
    loads[1].start()

    def slices(table, to, sem):
        def one(k, c):
            pltpu.make_async_copy(table.at[:, k, :], to.at[k], in_sem.at[sem]).start()
            return c

        lax.fori_loop(0, to.shape[0], one, 0)

    def arrive(to, sem):
        pltpu.make_async_copy(to, to, in_sem.at[sem]).wait()

    def rows_of(k, place):
        return pltpu.make_async_copy(sources.at[k], src_s[place], src_sem.at[place])

    barrier = pltpu.get_barrier_semaphore()

    def in_plane(j):
        other = lax.rem(place + j, nplane)
        return {"gx": lax.div(other, ngy), "gy": lax.rem(other, ngy)}

    def greet(device):
        pl.semaphore_signal(barrier, inc=1, device_id=device, device_id_type=MESH)

    def greet_plane(j, c):
        greet(in_plane(j))
        return c

    def greet_up(i, c):
        greet({"gz": i})
        return c

    pl.when(gz > 0)(lambda: greet({"gz": gz - 1}))
    lax.fori_loop(gz + 1, ngz, greet_up, 0)
    lax.fori_loop(1, nplane, greet_plane, 0)
    greeted = nplane - 1 + gz + (gz < ngz - 1).astype(jnp.int32)

    loads[0].wait()
    for b in range(ncell // 128):
        block = jnp.concatenate(
            [cells[:, b * 128 : (b + 1) * 128], jnp.zeros((128 - coef, 128), F32)], axis=0
        ).T
        own[b * 128 : (b + 1) * 128, :] = block
        pool[b * 128 : (b + 1) * 128, :] = block

    slices(up, up_v, 2)
    loads[2].start()
    loads[1].wait()
    neighbours = (
        (gx, ngx, lambda i: {"gx": i}),
        (gy, ngy, lambda i: {"gy": i}),
        (gz, ngz, lambda i: {"gz": i}),
    )

    def slot(i):
        return pool.at[pl.ds(ncell + i * nhalo, nhalo)]

    def face_copy(face, land, device):
        return pltpu.make_async_remote_copy(
            src_ref=faces.at[face],
            dst_ref=slot(land),
            send_sem=face_send.at[face],
            recv_sem=face_recv.at[land],
            device_id=device,
            device_id_type=MESH,
        )

    def gather_face(face):
        def part(i, c):
            for r in range(16):
                v = halo_s.at[face, pl.ds(i * 128 + r * 8, 8)]
                faces[face, pl.ds(pl.multiple_of(i * 128 + r * 8, 8), 8), :] = pick8(
                    own, lambda s: v[offs[s]], sub
                )
            return c

        lax.fori_loop(0, nhalo // 128, part, 0)

    for a, (at, count, device) in enumerate(neighbours):
        gather_face(2 * a)
        gather_face(2 * a + 1)
        if a == 0:
            pl.semaphore_wait(barrier, greeted)

        @pl.when(at < count - 1)
        def _():
            face_copy(2 * a + 1, 2 * a, device(at + 1)).start()

        @pl.when(at > 0)
        def _():
            face_copy(2 * a, 2 * a + 1, device(at - 1)).start()

    slices(down, down_v, 5)
    slices(m2l, m2l_v, 4)
    for k in range(4):
        rows_of(k, k).start()

    up_w[...] = jnp.zeros_like(up_w)
    arrive(up_v, 2)
    for o in range(8):
        hi, lo = split(up_v[o])
        up_w[0, 0:coef, o * 128 : o * 128 + coef] = hi
        up_w[1, 0:coef, o * 128 : o * 128 + coef] = lo

    def add_class(i, total):
        for r in range(16):
            total = total + own[pl.ds(pl.multiple_of(i * 128 + r * 8, 8), 8), :]
        return total

    classes = lax.fori_loop(0, ncell // 128, add_class, jnp.zeros((8, 128), F32))
    flat = jnp.concatenate([classes[o : o + 1, :] for o in range(8)], axis=1)
    box = dot3(jnp.broadcast_to(flat, (8, 1024)), up_w[0], up_w[1])
    mine[0] = box[0:1, :]

    def line_copy(sender, device):
        return pltpu.make_async_remote_copy(
            src_ref=mine.at[0],
            dst_ref=line.at[sender],
            send_sem=line_send.at[0],
            recv_sem=line_recv.at[sender],
            device_id={"gz": device},
            device_id_type=MESH,
        )

    def send_box(to, c):
        line_copy(gz, to).start()
        return c

    def get_box(sender, c):
        line_copy(sender, sender).wait_recv()
        return c

    line[gz] = box[0:1, :]

    for a, (at, count, _) in enumerate(neighbours):
        @pl.when(at == 0)
        def _():
            slot(2 * a)[...] = jnp.zeros((nhalo, 128), F32)

        @pl.when(at == count - 1)
        def _():
            slot(2 * a + 1)[...] = jnp.zeros((nhalo, 128), F32)

    for w in (down_w, side_w, near_w):
        w[...] = jnp.zeros_like(w)

    loads[2].wait()
    for a in range(3):
        for b in range(2):
            side_w[a, b, 0:coef, 0:coef] = side_v[a, :, b, :]
    merge = jnp.concatenate([side_w[0, 0], side_w[0, 1]], axis=1)
    merge_w[0], merge_w[1] = split(merge)
    four = nn3(jnp.concatenate([side_w[0, 0], side_w[0, 1]], axis=0), merge)
    merge4_w[0], merge4_w[1] = split(jnp.concatenate([four[0:128], four[128:256]], axis=1))
    levels = (ngz * nplane).bit_length() - 1
    turn = [lax.rem(lax.shift_right_logical(me, s), 2) for s in range(levels)]
    step = [side_w[2, turn[s]] for s in range(levels)]
    two = [nn3(step[s], step[s + 1]) for s in range(0, levels - 1, 2)]
    third = nn3(two[0], jnp.concatenate([step[2], two[1]], axis=1))
    rest = nn3(two[2], jnp.concatenate([step[6], two[3]], axis=1))
    upper = nn3(third[:, 128:256], jnp.concatenate([step[4], two[2], rest], axis=1))
    way = [None, step[0], two[0], third[:, 0:128], third[:, 128:256]]
    way += [upper[:, i * 128 : (i + 1) * 128] for i in range(4)]
    for s in range(levels):
        cross = side_w[1, turn[s]]
        far_w[0, :, s * 128 : (s + 1) * 128], far_w[1, :, s * 128 : (s + 1) * 128] = split(
            nn3(way[s], cross) if s else cross
        )
    arrive(down_v, 5)
    for o in range(8):
        hi, lo = split(down_v[o])
        down_w[0, o * 128 : o * 128 + coef, 0:coef] = hi
        down_w[1, o * 128 : o * 128 + coef, 0:coef] = lo
    acc[...] = jnp.zeros_like(acc)
    sibs[...] = jnp.zeros_like(sibs)

    def plane_copy(j):
        return pltpu.make_async_remote_copy(
            src_ref=mine.at[1],
            dst_ref=plane.at[place],
            send_sem=plane_send.at[0],
            recv_sem=plane_recv.at[0],
            device_id=in_plane(j),
            device_id_type=MESH,
        )

    def send_top(j, c):
        plane_copy(j).start()
        return c

    def all_of(buffer, count, send, recv):
        every = buffer.at[pl.ds(0, count - 1)]
        return pltpu.make_async_remote_copy(
            src_ref=every,
            dst_ref=every,
            send_sem=send.at[0],
            recv_sem=recv.at[0],
            device_id=in_plane(1),
            device_id_type=MESH,
        )

    def quads(count):
        rows = [boxes[pl.ds(i, count // 4, 4), :] for i in range(4)]
        return dot3(jnp.concatenate(rows, axis=1), merge4_w[0], merge4_w[1])

    def pair(index):
        return jnp.concatenate([boxes[pl.ds(2 * index, 1), :], boxes[pl.ds(2 * index + 1, 1), :]], axis=1)

    def merged(rows):
        return dot3(jnp.concatenate(rows, axis=0), merge_w[0], merge_w[1])

    def sibling(index, s):
        mask = lax.shift_right_logical(index, s)
        return mask + 1 - 2 * lax.rem(mask, 2)

    def line_done():
        lax.fori_loop(0, gz, get_box, 0)
        for i in range(ngz):
            boxes[i : i + 1, :] = line[i]
        sibs[0:1, :] = boxes[pl.ds(sibling(gz, 0), 1), :]
        first = pair(sibling(gz, 1))
        boxes[0:8, :] = quads(32)
        sibs[2:3, :] = boxes[pl.ds(sibling(gz, 2), 1), :]
        third = pair(sibling(gz, 3))
        boxes[0:2, :] = quads(8)
        sibs[4:5, :] = boxes[pl.ds(sibling(gz, 4), 1), :]
        top = merged([first, third, pair(0)])
        sibs[1:2, :] = top[0:1, :]
        sibs[3:4, :] = top[1:2, :]
        mine[1] = top[2:3, :]
        plane[place] = top[2:3, :]
        lax.fori_loop(1, nplane, send_top, 0)

    for a, (at, count, device) in enumerate(neighbours):
        @pl.when(at < count - 1)
        def _():
            face_copy(2 * a + 1, 2 * a, device(at + 1)).wait_send()
            face_copy(2 * a, 2 * a + 1, device(at + 1)).wait_recv()

        @pl.when(at > 0)
        def _():
            face_copy(2 * a, 2 * a + 1, device(at - 1)).wait_send()
            face_copy(2 * a + 1, 2 * a, device(at - 1)).wait_recv()


    def split_near(p, to):
        for h in range(2):
            hi, lo = split(m2l_v[p * 2 + h])
            near_w[to, 0:coef, h * 128 : h * 128 + coef] = hi
            near_w[to, 128 : 128 + coef, h * 128 : h * 128 + coef] = lo

    arrive(m2l_v, 4)
    split_near(0, 0)

    lax.fori_loop(0, gz, send_box, 0)

    def near_pair(p, half):
        def picked(h, n):
            return pick8(pool, lambda s: src_s[2 * half + h][n + s], sub)

        for h in range(2):
            rows_of(2 * p + h, 2 * half + h).wait()
        his, los = [], []
        for n in range(0, ncell, 16):
            rows = [jnp.concatenate([picked(h, n), picked(h, n + 8)], axis=0) for h in range(2)]
            hi, lo = split(jnp.concatenate(rows, axis=1))
            his.append(hi)
            los.append(lo)

        @pl.when(p + 2 < ops // 2)
        def _():
            for h in range(2):
                rows_of(2 * p + 4 + h, 2 * half + h).start()

        w = near_w[half]
        both = nt(jnp.concatenate(his, axis=0), w)
        low = nt(jnp.concatenate(los, axis=0), w[0:128])
        acc[...] += both[:, 0:128] + both[:, 128:256] + low
        split_near(jnp.minimum(p + 1, ops // 2 - 1), 1 - half)

    def hear_above():
        lax.fori_loop(gz + 1, ngz, get_box, 0)
        lax.fori_loop(gz + 1, ngz, send_box, 0)

    def near(i, c):
        for half in range(2):
            for pair_number, hook in ((UP_PAIR, hear_above), (LINE_PAIR, line_done)):
                if pair_number % 2 == half:
                    pl.when(i == pair_number // 2)(hook)
            near_pair(2 * i + half, half)
        return c

    lax.fori_loop(0, ops // 4, near, 0)

    all_of(plane, nplane, plane_send, plane_recv).wait()
    all_of(line, ngz, line_send, line_recv).wait_send()
    for i in range(nplane):
        boxes[i : i + 1, :] = plane[i]
    known_sibs = [sibs[s : s + 1, :] for s in range(5)]
    known_sibs.append(boxes[pl.ds(sibling(place, 0), 1), :])
    sixth = pair(sibling(place, 1))
    boxes[0:4, :] = quads(16)
    known_sibs.append(None)
    known_sibs.append(boxes[pl.ds(sibling(place, 2), 1), :])
    last = merged([sixth, pair(sibling(place, 3))])
    known_sibs[6] = last[0:1, :]
    known_sibs.append(last[1:2, :])
    every = jnp.concatenate(known_sibs, axis=1)
    g = dot3(every, far_w[0, :, 0 : levels * 128], far_w[1, :, 0 : levels * 128])
    spread = dot3(g, down_w[0], down_w[1])
    classes = jnp.concatenate([spread[0:1, o * 128 : (o + 1) * 128] for o in range(8)], axis=0)
    spread = jnp.concatenate([classes] * 16, axis=0).T
    for b in range(ncell // 128):
        block = acc[b * 128 : (b + 1) * 128, :].T + spread
        out[:, b * 128 : (b + 1) * 128] = block[0:coef, :]


def shards(mesh, multipoles, sources, halo_cells, m2l_ops, cell_up, cell_down, side_ops):
    coef, ncell = multipoles.shape
    ops = sources.shape[0]
    nhalo = halo_cells.shape[1]
    ngx, ngy, ngz = (mesh.shape[a] for a in AXES)
    nplane = ngx * ngy
    hbm = pl.BlockSpec(memory_space=pltpu.HBM)
    vmem, dma = pltpu.VMEM, pltpu.SemaphoreType.DMA
    m2l = jnp.transpose(m2l_ops, (1, 0, 2))
    up = jnp.transpose(cell_up, (1, 0, 2))
    down = jnp.transpose(cell_down, (1, 0, 2))
    side = jnp.transpose(side_ops, (0, 2, 1, 3))
    return pl.pallas_call(
        functools.partial(kernel, (coef, ncell, ops, nhalo, ngx, ngy, ngz)),
        out_shape=jax.ShapeDtypeStruct((coef, ncell), F32),
        in_specs=[hbm] * 7,
        out_specs=pl.BlockSpec(memory_space=vmem),
        scratch_shapes=[
            vmem((coef, ncell), F32),
            vmem((ncell, 128), F32),
            vmem((ncell + 6 * nhalo, 128), F32),
            vmem((6, nhalo, 128), F32),
            [pltpu.SMEM((ncell,), jnp.int32)] * 4,
            pltpu.SMEM((6, nhalo), jnp.int32),
            vmem((ops, coef, coef), F32),
            vmem((8, coef, coef), F32),
            vmem((8, coef, coef), F32),
            vmem((3, coef, 2, coef), F32),
            vmem((2, 256, 256), BF16),
            vmem((2, 128, 1024), BF16),
            vmem((2, 1024, 128), BF16),
            vmem((3, 2, 128, 128), F32),
            vmem((2, 128, 256), BF16),
            vmem((2, 128, 512), BF16),
            vmem((2, 128, 128 * 16), BF16),
            vmem((ncell, 128), F32),
            vmem((2, 1, 128), F32),
            vmem((ngz, 1, 128), F32),
            vmem((nplane, 1, 128), F32),
            vmem((ngz, 128), F32),
            vmem((16, 128), F32),
            dma((6,)),
            dma((4,)),
            dma((6,)),
            dma((6,)),
            dma((1,)),
            dma((ngz,)),
            dma((1,)),
            dma((1,)),
        ],
        compiler_params=pltpu.CompilerParams(
            collective_id=0, has_side_effects=True, vmem_limit_bytes=63 * 2**20
        ),
        cost_estimate=pl.CostEstimate(flops=3 * 10**9, bytes_accessed=4 * 10**6, transcendentals=0),
    )(multipoles, sources, halo_cells, m2l, up, down, side)


def solution(mesh):
    split_cells = P(None, AXES)
    split_rows = P(AXES, None)
    return jax.shard_map(
        functools.partial(shards, mesh),
        mesh=mesh,
        in_specs=(split_cells, split_rows, split_rows, P(), P(), P(), P()),
        out_specs=split_cells,
        check_vma=False,
    )
```
